128 devices in a mesh: batch: 8 (over x, z_lo), grid: 16 (over y, z_hi, core).
Axes of the slice: x: 4, y: 4, z: 4 (z_hi: 2, z_lo: 2; z = z_hi * 2 + z_lo), core: 2. Of those that a mesh axis runs over, the one named last changes fastest.
Arguments:
- samples: bfloat16 [8192, 1024], P('batch'), may hold values from -6 to 6
- point_index: int32 [2, 65536], P(None, 'grid'), may hold values from 0 to 8191
- targets: bfloat16 [8192, 65536], P('batch', 'grid'), may hold values from -6 to 6
- w_in: bfloat16 [1024, 256], replicated, may hold values from -0.1875 to 0.1875
- w_mid: bfloat16 [256, 256], replicated, may hold values from -0.375 to 0.375
- w_out: bfloat16 [256, 256], replicated, may hold values from -0.375 to 0.375
- v_in: bfloat16 [256, 256], replicated, may hold values from -0.375 to 0.375
- v_mid: bfloat16 [256, 256], replicated, may hold values from -0.375 to 0.375
- v_out: bfloat16 [256, 256], replicated, may hold values from -0.375 to 0.375
Outputs:
- grad_w_in: float32 [1024, 256], replicated
- grad_w_mid: float32 [256, 256], replicated
- grad_w_out: float32 [256, 256], replicated
- grad_v_in: float32 [256, 256], replicated
- grad_v_mid: float32 [256, 256], replicated
- grad_v_out: float32 [256, 256], replicated
- loss: float32 [], replicated
The draws below stay inside these ranges and needn't reach their ends.
All inputs are finite; a program needn't handle non-finite values.
Results may differ from the reference program's by a relative error of at most 0.004.
Values may be sent and summed in bfloat16 or wider, within the bound.
A program may use at most 128 MiB of HBM per device.

```python
import math
import jax
import jax.numpy as jnp
from jax import lax

M = 1024
H = 256
P_SIZE = 256
FEATS = 256
GRID_SIDE = 8192
SAMPLES = 8192
POINTS = 65536


def touch_ends(entries, own_key, smallest, top_value):
    shape = entries.shape
    spot = [jax.random.randint(jax.random.fold_in(own_key, axis), (), 0, shape[axis]) for axis in range(len(shape))]
    entries = entries.at[tuple(spot)].set(smallest)
    longest = shape.index(max(shape))
    spot[longest] = (spot[longest] + 1) % shape[longest]
    return entries.at[tuple(spot)].set(top_value)


def level_of(rng, extent, split, least, high):
    loudness, own = 1.0, jax.random.fold_in(rng, 6)
    for position, parts in split:
        steps = jnp.exp(jax.random.uniform(jax.random.fold_in(own, position), (parts,), jnp.float32, least / len(split), high / len(split)))
        loudness = loudness * jnp.repeat(steps, extent[position] // parts).reshape([-1 if axis == position else 1 for axis in range(len(extent))])
    return loudness


def normal_values(rng, shape, spread, bound, cuts=(), held_as=jnp.bfloat16):
    loudness = level_of(rng, shape, cuts, -0.22, 0.18) if cuts else 1.0
    result = jax.random.normal(rng, shape, jnp.float32) * spread * loudness
    return jnp.minimum(jnp.maximum(result, -bound), bound).astype(held_as)


def setup_inputs(seed: int = 0) -> dict:
    key_of = jax.random.split(jax.random.key(seed), 10)
    return {
        "samples": normal_values(key_of[0], (SAMPLES, M), 1.0, 6.0, ((0, 8),)),
        "point_index": touch_ends(jax.random.randint(key_of[1], (2, POINTS), 0, GRID_SIDE), jax.random.fold_in(key_of[1], 1), 0, GRID_SIDE - 1).astype(jnp.int32),
        "targets": normal_values(key_of[2], (SAMPLES, POINTS), 1.0, 6.0, ((0, 8), (1, 16))),
        "w_in": normal_values(key_of[3], (M, H), M ** -0.5, 0.1875),
        "w_mid": normal_values(key_of[4], (H, H), H ** -0.5, 0.375),
        "w_out": normal_values(key_of[5], (H, P_SIZE), H ** -0.5, 0.375),
        "v_in": normal_values(key_of[6], (FEATS, H), FEATS ** -0.5, 0.375),
        "v_mid": normal_values(key_of[7], (H, H), H ** -0.5, 0.375),
        "v_out": normal_values(key_of[8], (H, P_SIZE), H ** -0.5, 0.375),
    }


def fourier_features(point_index):
    quarter = FEATS // 4
    frequency = math.pi * (jnp.arange(quarter, dtype=jnp.float32) + 1.0)
    first_coord = (point_index[0].astype(jnp.float32) + 0.5) / GRID_SIDE
    second_coord = (point_index[1].astype(jnp.float32) + 0.5) / GRID_SIDE
    phase_one = first_coord[:, None] * frequency[None, :]
    phase_two = second_coord[:, None] * frequency[None, :]
    joined = jnp.concatenate([jnp.sin(phase_one), jnp.cos(phase_one), jnp.sin(phase_two), jnp.cos(phase_two)], axis=1)
    return joined.astype(jnp.bfloat16)

def contract_rows(left_side, right_side):
    return lax.dot_general(left_side, right_side, (((0,), (0,)), ((), ())), preferred_element_type=jnp.float32)

def contract_cols(left_side, right_side):
    return lax.dot_general(left_side, right_side, (((1,), (1,)), ((), ())), preferred_element_type=jnp.float32)

def network_forward(inputs, w_first, w_middle, w_last):
    hidden_one = jnp.tanh(jnp.dot(inputs, w_first, preferred_element_type=jnp.float32)).astype(jnp.bfloat16)
    hidden_two = jnp.tanh(jnp.dot(hidden_one, w_middle, preferred_element_type=jnp.float32)).astype(jnp.bfloat16)
    output = jnp.dot(hidden_two, w_last, preferred_element_type=jnp.float32).astype(jnp.bfloat16)
    return (hidden_one, hidden_two, output)

def network_backward(inputs, hidden_one, hidden_two, w_middle, w_last, out_grad):
    grad_last = contract_rows(hidden_two, out_grad)
    slope_two = 1.0 - jnp.square(hidden_two.astype(jnp.float32))
    back_two = (contract_cols(out_grad, w_last) * slope_two).astype(jnp.bfloat16)
    grad_middle = contract_rows(hidden_one, back_two)
    slope_one = 1.0 - jnp.square(hidden_one.astype(jnp.float32))
    back_one = (contract_cols(back_two, w_middle) * slope_one).astype(jnp.bfloat16)
    grad_first = contract_rows(inputs, back_one)
    return (grad_first, grad_middle, grad_last)

def reference(samples, point_index, targets, w_in, w_mid, w_out, v_in, v_mid, v_out):
    branch_one, branch_two, coeff = network_forward(samples, w_in, w_mid, w_out)
    trunk_input = fourier_features(point_index)
    trunk_one, trunk_two, basis = network_forward(trunk_input, v_in, v_mid, v_out)
    sample_count, point_count = targets.shape
    total_cells = sample_count * point_count
    width_scale = coeff.shape[1] ** (-0.5)
    grad_factor = 64.0 / math.sqrt(total_cells) * width_scale
    block_rows = math.gcd(sample_count, 512)
    block_count = sample_count // block_rows

    def visit_block(partial_value, blocks):
        basis_sum, square_sum = partial_value
        coeff_block, target_block = blocks
        predicted = contract_cols(coeff_block, basis) * width_scale
        residual = predicted - target_block.astype(jnp.float32)
        pred_grad = (residual * grad_factor).astype(jnp.bfloat16)
        coeff_part = jnp.dot(pred_grad, basis, preferred_element_type=jnp.float32)
        basis_sum = basis_sum + contract_rows(pred_grad, coeff_block)
        square_sum = square_sum + jnp.sum(residual * residual)
        return ((basis_sum, square_sum), coeff_part)
    initial = (jnp.zeros(basis.shape, jnp.float32), jnp.zeros((), jnp.float32))
    blocks = (coeff.reshape(block_count, block_rows, coeff.shape[1]), targets.reshape(block_count, block_rows, point_count))
    (basis_sum, square_sum), coeff_parts = lax.scan(visit_block, initial, blocks)
    coeff_grad = coeff_parts.reshape(sample_count, coeff.shape[1]).astype(jnp.bfloat16)
    basis_grad = basis_sum.astype(jnp.bfloat16)
    grad_w_in, grad_w_mid, grad_w_out = network_backward(samples, branch_one, branch_two, w_mid, w_out, coeff_grad)
    grad_v_in, grad_v_mid, grad_v_out = network_backward(trunk_input, trunk_one, trunk_two, v_mid, v_out, basis_grad)
    loss = square_sum / (2.0 * total_cells)
    return (grad_w_in, grad_w_mid, grad_w_out, grad_v_in, grad_v_mid, grad_v_out, loss)
```

```python
import functools
import math

import jax
import jax.numpy as jnp
from jax import lax
from jax.experimental import pallas as pl
from jax.experimental.pallas import tpu as pltpu
from jax.sharding import PartitionSpec as P

MESH = pl.DeviceIdType.MESH
BF = jnp.bfloat16
F32 = jnp.float32

GRID_SIDE = 8192
S0, S1, S2, S3 = 6.283164044266556, -41.33714236534519, 81.34076866645029, -70.99343091074333
ROUNDER = 12582912.0

PLANE = 16
LINE = 4
BRANCH_ROWS = 64
TRUNK_ROWS = 32


def dot(left, right, left_dim, right_dim):
    return lax.dot_general(
        left, right, (((left_dim,), (right_dim,)), ((), ())), preferred_element_type=F32
    )


def wave(phase):
    turn = phase - ((phase + ROUNDER) - ROUNDER)
    y = 0.25 - jnp.abs(turn)
    sq = y * y
    return y * (S0 + sq * (S1 + sq * (S2 + sq * S3)))


def coords():
    b = lax.axis_index("batch")
    g = lax.axis_index("grid")
    return b // 2, g // 4, ((g // 2) % 2) * 2 + b % 2, g % 2


def device(x, y, z, core):
    return {"batch": x * 2 + z % 2, "grid": y * 4 + (z // 2) * 2 + core}


def remote(src, dst, sems, k, target):
    return pltpu.make_async_remote_copy(
        src_ref=src,
        dst_ref=dst,
        send_sem=sems.at[0, k],
        recv_sem=sems.at[1, k],
        device_id=target,
        device_id_type=MESH,
    )


def wait_bytes(ref, sem):
    pltpu.make_async_copy(ref, ref, sem).wait()


class Reducer:
    def __init__(self, own, pair, send, recv, line, gathered, sems, rows, out_rows, has_loss):
        self.own, self.pair, self.send, self.recv = own, pair, send, recv
        self.line, self.gathered, self.sems = line, gathered, sems
        self.rows, self.out_rows, self.has_loss = rows, out_rows, has_loss
        self.x, self.y, self.z, self.core = coords()
        self.rank = self.y * 4 + self.z

    def peer(self, offset):
        t = (self.rank + offset) % PLANE
        return t, device(self.x, t // 4, t % 4, self.core)

    def sibling(self):
        return device(self.x, self.y, self.z, 1 - self.core)

    def start_pair(self):
        remote(self.own.at[1 - self.core], self.pair, self.sems, 0, self.sibling()).start()

    def start_plane(self):
        wait_bytes(self.pair, self.sems.at[1, 0])
        for m in range(PLANE):
            both = self.own[self.core, m] + self.pair[m]
            self.send[m] = both.astype(BF)
            if self.has_loss:
                square = both[48:56]
                high = square.astype(BF).astype(F32)
                self.send[m, 48:64] = jnp.concatenate([high, square - high], axis=0).astype(BF)
        self.recv[self.rank] = self.send[self.rank]

        @pl.loop(1, PLANE, unroll=True)
        def _(offset):
            t, target = self.peer(offset)
            remote(self.send.at[t], self.recv.at[self.rank], self.sems, 1, target).start()

    def start_line(self):
        wait_bytes(self.recv.at[pl.ds(0, PLANE - 1)], self.sems.at[1, 1])
        total = self.recv[0].astype(F32)
        for m in range(1, PLANE):
            total = total + self.recv[m].astype(F32)
        self.line[self.x] = total
        for offset in range(1, LINE):
            target = device((self.x + offset) % LINE, self.y, self.z, self.core)
            slot = self.line.at[self.x]
            remote(slot, slot, self.sems, 2, target).start()

    def start_gather(self):
        wait_bytes(self.line.at[pl.ds(0, LINE - 1)], self.sems.at[1, 2])
        total = (self.line[0] + self.line[1]) + (self.line[2] + self.line[3])
        self.gathered[self.core, self.rank] = total[: self.out_rows].astype(BF)
        slot = self.gathered.at[self.core, self.rank]

        @pl.loop(1, PLANE, unroll=True)
        def _(offset):
            _, target = self.peer(offset)
            remote(slot, slot, self.sems, 3, target).start()

        return total

    def start_return(self):
        half = self.gathered.at[self.core]
        wait_bytes(half.at[pl.ds(0, PLANE - 1)], self.sems.at[1, 3])
        remote(half, half, self.sems, 4, self.sibling()).start()

    def finish(self):
        wait_bytes(self.gathered.at[0], self.sems.at[1, 4])
        wait_bytes(self.pair, self.sems.at[0, 0])
        wait_bytes(self.send.at[pl.ds(0, PLANE - 1)], self.sems.at[0, 1])
        wait_bytes(self.line.at[pl.ds(0, LINE - 1)], self.sems.at[0, 2])
        wait_bytes(self.gathered.at[0, pl.ds(0, PLANE - 1)], self.sems.at[0, 3])
        wait_bytes(self.gathered.at[0], self.sems.at[0, 4])


def step_kernel(
    grad_factor,
    samples_in, index_in, targets_in, w_in_in, w_mid_in, w_out_in, v_in_in, v_mid_in, v_out_in,
    branch_out, trunk_out, loss_out,
    samples, index, targets, w_in, w_mid, w_out, v_in, v_mid, v_out,
    feats, t_one, t_two, basis, basis_grad, b_one, b_two, coeff, coeff_t, coeff_grad,
    squares,
    branch_own, branch_pair, branch_send, branch_recv, branch_line,
    trunk_own, trunk_pair, trunk_send, trunk_recv, trunk_line,
    local_sems, target_sems, branch_sems, trunk_sems,
):
    samp, pts = targets.shape
    chunks = target_sems.shape[0]
    chunk = samp // chunks
    x, y, z, core = coords()
    rank = y * 4 + z

    loads = []
    for k, (src, dst) in enumerate(
        (
            (index_in, index), (v_in_in, v_in), (v_mid_in, v_mid), (v_out_in, v_out),
            (w_in_in, w_in), (w_mid_in, w_mid), (w_out_in, w_out), (samples_in, samples),
        )
    ):
        copy = pltpu.make_async_copy(src, dst, local_sems.at[k])
        copy.start()
        loads.append(copy)
    target_loads = []
    for k in range(chunks):
        rows = pl.ds(k * chunk, chunk)
        copy = pltpu.make_async_copy(targets_in.at[rows], targets.at[rows], target_sems.at[k])
        copy.start()
        target_loads.append(copy)

    barrier = pltpu.get_barrier_semaphore()

    def greet(target):
        pl.semaphore_signal(barrier, inc=1, device_id=target, device_id_type=MESH)

    greet(device(x, y, z, 1 - core))
    for offset in range(1, LINE):
        greet(device((x + offset) % LINE, y, z, core))

    @pl.loop(1, PLANE)
    def _(offset):
        t = (rank + offset) % PLANE
        greet(device(x, t // 4, t % 4, core))

    for k in range(4):
        loads[k].wait()
    quarter = feats.shape[0] // 4
    order = lax.broadcasted_iota(jnp.int32, (quarter, 1), 0).astype(F32) + 1.0
    v_in_t, v_mid_t, v_out_t = v_in[...].T, v_mid[...].T, v_out[...].T
    wide = 1024
    for p in range(0, pts, wide):
        cols = pl.ds(p, wide)
        for axis in range(2):
            spot = index[axis : axis + 1, cols].astype(F32)
            phase = order * ((2.0 * spot + 1.0) * (0.25 / GRID_SIDE))
            base = 2 * axis * quarter
            feats[base : base + quarter, cols] = wave(phase - 0.25).astype(BF)
            feats[base + quarter : base + 2 * quarter, cols] = wave(phase).astype(BF)
        t_one[:, cols] = jnp.tanh(dot(v_in_t, feats[:, cols], 1, 0)).astype(BF)
        t_two[:, cols] = jnp.tanh(dot(v_mid_t, t_one[:, cols], 1, 0)).astype(BF)
        basis[:, cols] = dot(v_out_t, t_two[:, cols], 1, 0).astype(BF)

    for k in range(4, 8):
        loads[k].wait()
    b_one[...] = jnp.tanh(dot(samples[...], w_in[...], 1, 0)).astype(BF)
    b_two[...] = jnp.tanh(dot(b_one[...], w_mid[...], 1, 0)).astype(BF)
    coeff[...] = dot(b_two[...], w_out[...], 1, 0).astype(BF)
    coeff_t[...] = coeff[...].T

    squares[...] = jnp.zeros_like(squares)
    for k in range(chunks):
        rows = pl.ds(k * chunk, chunk)
        target_loads[k].wait()
        scaled = coeff[rows, :] * jnp.asarray(1.0 / 16.0, BF)
        for p in range(0, pts, wide):
            cols = pl.ds(p, wide)
            residual = dot(scaled, basis[:, cols], 1, 0) - targets[rows, cols].astype(F32)
            targets[rows, cols] = (residual * grad_factor).astype(BF)
            square = residual * residual
            squares[...] += jnp.sum(square.reshape(chunk // 8, 8, wide), axis=0)
        coeff_grad[rows, :] = dot(targets[rows, :], basis[...], 1, 1).astype(BF)

    grad = coeff_grad[...]
    part_out = dot(b_two[...], grad, 0, 0)
    slope = 1.0 - jnp.square(b_two[...].astype(F32))
    back_two = (dot(grad, w_out[...], 1, 1) * slope).astype(BF)
    part_mid = dot(b_one[...], back_two, 0, 0)
    slope = 1.0 - jnp.square(b_one[...].astype(F32))
    back_one = (dot(back_two, w_mid[...], 1, 1) * slope).astype(BF)
    part_in = dot(samples[...], back_one, 0, 0)
    square = jnp.sum(squares[...].reshape(8, wide // 128, 128), axis=1)
    square = jnp.concatenate([square, jnp.zeros_like(square)], axis=1)
    for m in range(2 * PLANE):
        c, r = m // PLANE, m % PLANE
        branch_own[c, r, 0:32] = part_in[m * 32 : m * 32 + 32]
        branch_own[c, r, 32:40] = part_mid[m * 8 : m * 8 + 8]
        branch_own[c, r, 40:48] = part_out[m * 8 : m * 8 + 8]
        branch_own[c, r, 48:56] = square
        branch_own[c, r, 56:64] = jnp.zeros_like(square)

    branch = Reducer(
        branch_own, branch_pair, branch_send, branch_recv, branch_line, branch_out,
        branch_sems, BRANCH_ROWS, 48, True,
    )
    trunk = Reducer(
        trunk_own, trunk_pair, trunk_send, trunk_recv, trunk_line, trunk_out,
        trunk_sems, TRUNK_ROWS, 32, False,
    )

    pl.semaphore_wait(barrier, PLANE + LINE - 1)
    branch.start_pair()

    def basis_columns(p):
        cols = pl.ds(p, wide)
        basis_grad[:, cols] = dot(coeff_t[...], targets[:, cols], 1, 0).astype(BF)

    for p in range(0, pts // 2, wide):
        basis_columns(p)
    branch.start_plane()
    for p in range(pts // 2, pts, wide):
        basis_columns(p)

    for p in range(0, pts, wide):
        cols = pl.ds(p, wide)
        grad = basis_grad[:, cols]
        last = dot(t_two[:, cols], grad, 1, 1)
        slope = 1.0 - jnp.square(t_two[:, cols].astype(F32))
        back_two = (dot(v_out[...], grad, 1, 0) * slope).astype(BF)
        middle = dot(t_one[:, cols], back_two, 1, 1)
        slope = 1.0 - jnp.square(t_one[:, cols].astype(F32))
        back_one = (dot(v_mid[...], back_two, 1, 0) * slope).astype(BF)
        first = dot(feats[:, cols], back_one, 1, 1)
        if p == 0:
            part_first, part_middle, part_last = first, middle, last
        else:
            part_first, part_middle, part_last = (
                part_first + first, part_middle + middle, part_last + last,
            )
    for m in range(2 * PLANE):
        c, r = m // PLANE, m % PLANE
        trunk_own[c, r, 0:8] = part_first[m * 8 : m * 8 + 8]
        trunk_own[c, r, 8:16] = part_middle[m * 8 : m * 8 + 8]
        trunk_own[c, r, 16:24] = part_last[m * 8 : m * 8 + 8]
        trunk_own[c, r, 24:32] = jnp.zeros((8, 256), F32)
    trunk.start_pair()
    branch.start_line()
    trunk.start_plane()
    square = branch.start_gather()[48:64]
    square = square[0:8] + square[8:16]
    loss_out[...] = jnp.sum(square, keepdims=True)
    trunk.start_line()
    trunk.start_gather()
    branch.start_return()
    trunk.start_return()
    branch.finish()
    trunk.finish()


def spread_kernel(
    loss_scale, branch, trunk, square, g_w_in, g_w_mid, g_w_out, g_v_in, g_v_mid, g_v_out, loss
):
    for m in range(2 * PLANE):
        c, r = m // PLANE, m % PLANE
        part = branch[c, r].astype(F32)
        g_w_in[m * 32 : m * 32 + 32] = part[0:32]
        g_w_mid[m * 8 : m * 8 + 8] = part[32:40]
        g_w_out[m * 8 : m * 8 + 8] = part[40:48]
        part = trunk[c, r].astype(F32)
        g_v_in[m * 8 : m * 8 + 8] = part[0:8]
        g_v_mid[m * 8 : m * 8 + 8] = part[8:16]
        g_v_out[m * 8 : m * 8 + 8] = part[16:24]
    loss[...] = square[...] * loss_scale


def on_device(samples, point_index, targets, w_in, w_mid, w_out, v_in, v_mid, v_out):
    samp, pts = targets.shape
    total_cells = samp * lax.axis_size("batch") * pts * lax.axis_size("grid")
    sensors, hidden = w_in.shape
    grad_factor = 64.0 / math.sqrt(total_cells) * w_out.shape[1] ** (-0.5)
    chunks = 4
    any_spec = pl.BlockSpec(memory_space=pl.ANY)
    vmem = pl.BlockSpec(memory_space=pltpu.VMEM)
    inputs = (samples, point_index, targets, w_in, w_mid, w_out, v_in, v_mid, v_out)
    v = pltpu.VMEM
    scratch = [v(a.shape, a.dtype) for a in inputs]
    scratch += [v((hidden, pts), BF)] * 5
    scratch += [v((samp, hidden), BF)] * 3 + [v((hidden, samp), BF), v((samp, hidden), BF)]
    scratch += [v((8, 1024), F32)]
    for rows in (BRANCH_ROWS, TRUNK_ROWS):
        scratch += [
            v((2, PLANE, rows, 256), F32),
            v((PLANE, rows, 256), F32),
            v((PLANE, rows, 256), BF),
            v((PLANE, rows, 256), BF),
            v((LINE, rows, 256), F32),
        ]
    scratch += [
        pltpu.SemaphoreType.DMA((8,)),
        pltpu.SemaphoreType.DMA((chunks,)),
        pltpu.SemaphoreType.DMA((2, 5)),
        pltpu.SemaphoreType.DMA((2, 5)),
    ]
    branch, trunk, square = pl.pallas_call(
        functools.partial(step_kernel, grad_factor),
        out_shape=(
            jax.ShapeDtypeStruct((2, PLANE, 48, 256), BF),
            jax.ShapeDtypeStruct((2, PLANE, TRUNK_ROWS, 256), BF),
            jax.ShapeDtypeStruct((1, 1), F32),
        ),
        in_specs=[any_spec] * 9,
        out_specs=[vmem] * 3,
        scratch_shapes=scratch,
        compiler_params=pltpu.CompilerParams(
            collective_id=0, has_side_effects=True, vmem_limit_bytes=58 << 20
        ),
        name="deeponet_step",
    )(*inputs)
    shapes = [(sensors, hidden)] + [(hidden, hidden)] * 5 + [(1, 1)]
    outs = pl.pallas_call(
        functools.partial(spread_kernel, 1.0 / (2.0 * total_cells)),
        out_shape=[jax.ShapeDtypeStruct(s, F32) for s in shapes],
        in_specs=[vmem] * 3,
        out_specs=[vmem] * 7,
        compiler_params=pltpu.CompilerParams(vmem_limit_bytes=32 << 20),
        name="spread_gradients",
    )(branch, trunk, square)
    return (*outs[:6], outs[6].reshape(()))


def solution(mesh):
    placed = (P("batch", None), P(None, "grid"), P("batch", "grid"), P(), P(), P(), P(), P(), P())
    return jax.shard_map(
        on_device,
        mesh=mesh,
        in_specs=placed,
        out_specs=(P(), P(), P(), P(), P(), P(), P()),
        check_vma=False,
    )
```

```python
import functools
import itertools
import math

import jax
import jax.numpy as jnp
from jax import lax
from jax.experimental import pallas as pl
from jax.experimental.pallas import tpu as pltpu
from jax.sharding import PartitionSpec as P

MESH = pl.DeviceIdType.MESH
BF = jnp.bfloat16
F32 = jnp.float32

GRID_SIDE = 8192
S0, S1, S2, S3, S4 = (
    6.283185160089221, -41.34165503135105, 81.60100406887733, -76.54978218664795, 39.536705209824365,
)
ROUNDER = 12582912.0

CHIPS = 64
TILE = (16, 128)
BRANCH_TILES, TRUNK_TILES = 96, 64
LOSS_TILE = 48


def dot(left, right, left_dim, right_dim):
    return lax.dot_general(
        left, right, (((left_dim,), (right_dim,)), ((), ())), preferred_element_type=F32
    )


def wave(phase):
    turn = phase - ((phase + ROUNDER) - ROUNDER)
    y = 0.25 - jnp.abs(turn)
    sq = y * y
    return y * (S0 + sq * (S1 + sq * (S2 + sq * (S3 + sq * S4))))


def waves(turns, count):
    order = lax.broadcasted_iota(jnp.int32, (8, 1), 0).astype(F32) + 1.0
    phase = order * turns
    sines, cosines = [wave(phase - 0.25)], [wave(phase)]
    while len(sines) * 8 < count:
        by_sin, by_cos = sines[-1][7:8], cosines[-1][7:8]
        pairs = list(zip(sines, cosines))
        sines += [s * by_cos + c * by_sin for s, c in pairs]
        cosines += [c * by_cos - s * by_sin for s, c in pairs]
    return jnp.concatenate(sines, axis=0), jnp.concatenate(cosines, axis=0)


def halves(square):
    high = square.astype(BF).astype(F32)
    return jnp.concatenate([high, square - high], axis=0).astype(BF)


def coords():
    b = lax.axis_index("batch")
    g = lax.axis_index("grid")
    return b // 2, g // 4, ((g // 2) % 2) * 2 + b % 2, g % 2


def device(x, y, z, core):
    return {"batch": x * 2 + z % 2, "grid": y * 4 + (z // 2) * 2 + core}


def remote(src, dst, sems, k, target):
    return pltpu.make_async_remote_copy(
        src_ref=src,
        dst_ref=dst,
        send_sem=sems.at[0, k],
        recv_sem=sems.at[1, k],
        device_id=target,
        device_id_type=MESH,
    )


def wait_bytes(ref, sem):
    pltpu.make_async_copy(ref, ref, sem).wait()


OFFSETS = sorted(
    (o for o in itertools.product(range(4), repeat=3) if any(o)),
    key=lambda o: -sum(min(d, 4 - d) for d in o),
)


def chip_tiles(rank, doubled):
    if not doubled:
        return rank, 1
    even = (rank // 16 + rank // 4 + rank) % 2 == 0
    return 3 * (rank // 2) + (rank % 2) * (1 if even else 2), 2 if even else 1


class Reducer:
    def __init__(self, own, pair_send, pair_recv, send, recv, result, gathered, sems, doubled):
        self.own, self.pair_send, self.pair_recv = own, pair_send, pair_recv
        self.send, self.recv, self.result, self.gathered = send, recv, result, gathered
        self.sems, self.doubled = sems, doubled
        self.tiles = own.shape[1]
        self.x, self.y, self.z, self.core = coords()
        self.rank = (self.x * 4 + self.y) * 4 + self.z
        self.odd = (self.x + self.y + self.z) % 2
        xs = [(self.x + d) % 4 for d in range(4)]
        ys = [(self.y + d) % 4 for d in range(4)]
        zs = [(self.z + d) % 4 for d in range(4)]
        ranks = [x * 16 for x in xs], [y * 4 for y in ys], zs
        batches = [x * 2 for x in xs], [z % 2 for z in zs]
        grids = [y * 4 + self.core for y in ys], [(z // 2) * 2 for z in zs]
        self.others = [
            (
                sum(o) % 2,
                ranks[0][o[0]] + ranks[1][o[1]] + ranks[2][o[2]],
                {"batch": batches[0][o[0]] + batches[1][o[2]], "grid": grids[0][o[1]] + grids[1][o[2]]},
            )
            for o in OFFSETS
        ]

    def by_parity(self, action):
        if self.doubled:
            pl.when(self.odd == 0)(lambda: action(0))
            pl.when(self.odd == 1)(lambda: action(1))
        else:
            action(0)

    def place(self, rank, odd):
        if not self.doubled:
            return rank, 1
        return 3 * (rank // 2) + (rank % 2) * (1 + odd), 2 - odd

    def sibling(self):
        return device(self.x, self.y, self.z, 1 - self.core)

    def start_pair(self, square=None):
        self.pair_send[...] = self.own[1 - self.core].astype(BF)
        if square is not None:
            self.pair_send[LOSS_TILE] = halves(square)
        remote(self.pair_send, self.pair_recv, self.sems, 0, self.sibling()).start()

    def start_scatter(self, square=None):
        wait_bytes(self.pair_recv, self.sems.at[1, 0])
        self.send[...] = (self.own[self.core] + self.pair_recv[...].astype(F32)).astype(BF)
        if square is not None:
            both = self.pair_recv[LOSS_TILE].astype(F32)
            self.send[LOSS_TILE] = halves(square + (both[:8] + both[8:]))

        def go(odd):
            spot, count = self.place(self.rank, odd)
            for k in range(count):
                self.recv[k, self.rank] = self.send[spot + k]
            for turn, rank, target in self.others:
                spot, count = self.place(rank, (odd + turn) % 2)
                src = self.send.at[pl.ds(spot, count)]
                dst = self.recv.at[pl.ds(0, count), self.rank]
                remote(src, dst, self.sems, 1, target).start()

        self.by_parity(go)

    def start_gather(self, has_square=False):
        def go(odd):
            spot, count = self.place(self.rank, odd)
            wait_bytes(self.recv.at[pl.ds(0, count), pl.ds(0, CHIPS - 1)], self.sems.at[1, 1])
            for k in range(count):
                total = jnp.sum(self.recv[k].astype(F32), axis=0)
                sent = total.astype(BF)
                if has_square:
                    sent = jnp.where(self.rank == LOSS_TILE, halves(total[:8] + total[8:]), sent)
                self.result[k] = sent
            src = self.result.at[pl.ds(0, count)]
            dst = self.gathered.at[self.core, pl.ds(spot, count)]
            for _, _, target in self.others:
                remote(src, dst, self.sems, 3, target).start()
            pltpu.make_async_copy(src, dst, self.sems.at[0, 5]).start()

        self.by_parity(go)

    def start_return(self):
        half = self.gathered.at[self.core]

        def go(odd):
            spot, count = self.place(self.rank, odd)
            wait_bytes(self.result.at[pl.ds(0, count)], self.sems.at[0, 5])
            wait_bytes(self.send.at[pl.ds(0, self.tiles - count)], self.sems.at[1, 3])

        self.by_parity(go)
        remote(half, half, self.sems, 4, self.sibling()).start()

    def finish(self):
        wait_bytes(self.pair_send, self.sems.at[0, 0])

        def go(odd):
            _, count = self.place(self.rank, odd)
            wait_bytes(self.send.at[pl.ds(0, self.tiles - count)], self.sems.at[0, 1])
            wait_bytes(self.recv.at[pl.ds(0, count), pl.ds(0, CHIPS - 1)], self.sems.at[0, 3])

        self.by_parity(go)
        wait_bytes(self.pair_send, self.sems.at[0, 4])
        wait_bytes(self.pair_recv, self.sems.at[1, 4])


def tile_spots():
    places = [chip_tiles(r, True) for r in range(CHIPS)]
    return [s for s, _ in places], [s + 1 for s, n in places if n == 2]


def step_kernel(
    grad_factor,
    samples_in, index_in, targets_in, w_in_in, w_mid_in, w_out_in, v_in_in, v_mid_in, v_out_in,
    branch_out, trunk_out,
    samples, index, targets, w_in, w_mid, w_out, v_in, v_mid, v_out,
    feats, t_one, t_two, basis, basis_grad, b_one, b_two, coeff, coeff_t, coeff_grad,
    squares,
    branch_own, branch_pair_send, branch_pair_recv, branch_send, branch_recv, branch_result,
    trunk_own, trunk_pair_send, trunk_pair_recv, trunk_send, trunk_recv, trunk_result,
    local_sems, target_sems, branch_sems, trunk_sems,
):
    samp, pts = targets.shape
    chunks = target_sems.shape[0]
    chunk = samp // chunks
    branch = Reducer(
        branch_own, branch_pair_send, branch_pair_recv, branch_send, branch_recv, branch_result,
        branch_out, branch_sems, True,
    )
    trunk = Reducer(
        trunk_own, trunk_pair_send, trunk_pair_recv, trunk_send, trunk_recv, trunk_result,
        trunk_out, trunk_sems, False,
    )

    loads = []
    for k, (src, dst) in enumerate(
        (
            (index_in, index), (v_in_in, v_in), (v_mid_in, v_mid), (v_out_in, v_out),
            (w_in_in, w_in), (w_mid_in, w_mid), (w_out_in, w_out), (samples_in, samples),
        )
    ):
        copy = pltpu.make_async_copy(src, dst, local_sems.at[k])
        copy.start()
        loads.append(copy)
    target_loads = []
    for k in range(chunks):
        rows = pl.ds(k * chunk, chunk)
        copy = pltpu.make_async_copy(targets_in.at[rows], targets.at[rows], target_sems.at[k])
        copy.start()
        target_loads.append(copy)

    barrier = pltpu.get_barrier_semaphore()

    def greet(target):
        pl.semaphore_signal(barrier, inc=1, device_id=target, device_id_type=MESH)

    greet(trunk.sibling())
    for _, _, target in trunk.others:
        greet(target)

    for k in range(4):
        loads[k].wait()
    quarter = feats.shape[0] // 4
    v_in_t, v_mid_t, v_out_t = v_in[...].T, v_mid[...].T, v_out[...].T
    wide = 1024
    block = 512
    blocks = pts // block

    def trunk_feats(p):
        cols = pl.ds(p * block, block)
        for axis in range(2):
            turns = (2.0 * index[axis : axis + 1, cols].astype(F32) + 1.0) * (0.25 / GRID_SIDE)
            sines, cosines = waves(turns, quarter)
            base = 2 * axis * quarter
            feats[base : base + quarter, cols] = sines.astype(BF)
            feats[base + quarter : base + 2 * quarter, cols] = cosines.astype(BF)

    def trunk_one(p):
        cols = pl.ds(p * block, block)
        t_one[:, cols] = jnp.tanh(dot(v_in_t, feats[:, cols], 1, 0)).astype(BF)

    def trunk_two(p):
        cols = pl.ds(p * block, block)
        t_two[:, cols] = jnp.tanh(dot(v_mid_t, t_one[:, cols], 1, 0)).astype(BF)

    def trunk_basis(p):
        cols = pl.ds(p * block, block)
        basis[:, cols] = dot(v_out_t, t_two[:, cols], 1, 0).astype(BF)

    quarter_rows = samp // 4

    def branch_one(k):
        rows = pl.ds(k * quarter_rows, quarter_rows)
        b_one[rows, :] = jnp.tanh(dot(samples[rows, :], w_in[...], 1, 0)).astype(BF)

    def branch_two(k):
        rows = pl.ds(k * quarter_rows, quarter_rows)
        b_two[rows, :] = jnp.tanh(dot(b_one[rows, :], w_mid[...], 1, 0)).astype(BF)

    def branch_coeff(k):
        rows = pl.ds(k * quarter_rows, quarter_rows)
        coeff[rows, :] = dot(b_two[rows, :], w_out[...], 1, 0).astype(BF)

    stages = (trunk_feats, trunk_one, trunk_two, trunk_basis)
    branch_stages = (branch_one, branch_two, branch_coeff)
    branch_from = 5
    for step in range(blocks + len(stages) - 1):
        if step == branch_from:
            for k in range(4, 8):
                loads[k].wait()
        for lag, stage in enumerate(stages):
            if 0 <= step - lag < blocks:
                stage(step - lag)
        for lag, stage in enumerate(branch_stages):
            if 0 <= step - branch_from - lag < 4:
                stage(step - branch_from - lag)
    coeff_t[...] = coeff[...].T

    squares[...] = jnp.zeros_like(squares)
    for k in range(chunks):
        rows = pl.ds(k * chunk, chunk)
        target_loads[k].wait()
        scaled = coeff[rows, :] * jnp.asarray(1.0 / 16.0, BF)
        for p in range(0, pts, wide):
            cols = pl.ds(p, wide)
            residual = dot(scaled, basis[:, cols], 1, 0) - targets[rows, cols].astype(F32)
            targets[rows, cols] = (residual * grad_factor).astype(BF)
            square = residual * residual
            squares[...] += jnp.sum(square.reshape(chunk // 8, 8, wide), axis=0)
        coeff_grad[rows, :] = dot(targets[rows, :], basis[...], 1, 1).astype(BF)

    grad = coeff_grad[...]
    part_out = dot(b_two[...], grad, 0, 0)
    slope = 1.0 - jnp.square(b_two[...].astype(F32))
    back_two = (dot(grad, w_out[...], 1, 1) * slope).astype(BF)
    part_mid = dot(b_one[...], back_two, 0, 0)
    slope = 1.0 - jnp.square(b_one[...].astype(F32))
    back_one = (dot(back_two, w_mid[...], 1, 1) * slope).astype(BF)
    part_in = dot(samples[...], back_one, 0, 0)
    square = jnp.sum(squares[...].reshape(8, wide // 128, 128), axis=1)

    def pack(own, part, core, spots, row):
        for k, spot in enumerate(spots):
            strip = part[row + 8 * k : row + 8 * k + 8]
            own[core, spot, 0:8] = strip[:, :128]
            own[core, spot, 8:16] = strip[:, 128:]

    singles, doubles = tile_spots()
    for c in range(2):
        pack(branch_own, part_in, c, singles, c * 512)
        pack(branch_own, part_mid, c, doubles[:16], c * 128)
        pack(branch_own, part_out, c, doubles[16:], c * 128)

    pl.semaphore_wait(barrier, CHIPS)
    branch.start_pair()

    def basis_columns(p):
        cols = pl.ds(p, wide)
        basis_grad[:, cols] = dot(coeff_t[...], targets[:, cols], 1, 0).astype(BF)

    for p in range(0, pts // 2, wide):
        basis_columns(p)
    branch.start_scatter()
    for p in range(pts // 2, pts, wide):
        basis_columns(p)

    for p in range(0, pts, wide):
        cols = pl.ds(p, wide)
        grad = basis_grad[:, cols]
        last = dot(t_two[:, cols], grad, 1, 1)
        slope = 1.0 - jnp.square(t_two[:, cols].astype(F32))
        back_two = (dot(v_out[...], grad, 1, 0) * slope).astype(BF)
        middle = dot(t_one[:, cols], back_two, 1, 1)
        slope = 1.0 - jnp.square(t_one[:, cols].astype(F32))
        back_one = (dot(v_mid[...], back_two, 1, 0) * slope).astype(BF)
        first = dot(feats[:, cols], back_one, 1, 1)
        if p == 0:
            part_first, part_middle, part_last = first, middle, last
        else:
            part_first, part_middle, part_last = (
                part_first + first, part_middle + middle, part_last + last,
            )
    for c in range(2):
        for k, part in enumerate((part_first, part_middle, part_last)):
            pack(trunk_own, part, c, range(16 * k, 16 * k + 16), c * 128)
        trunk_own[c, LOSS_TILE:] = jnp.zeros((TRUNK_TILES - LOSS_TILE, *TILE), F32)
    trunk.start_pair(square)
    trunk.start_scatter(square)
    branch.start_gather()
    trunk.start_gather(has_square=True)
    branch.start_return()
    trunk.start_return()
    branch.finish()
    trunk.finish()


def spread_kernel(
    loss_scale, branch_in, trunk_in, g_w_in, g_w_mid, g_w_out, g_v_in, g_v_mid, g_v_out, loss,
    branch, trunk, w_in, w_mid, w_out, v_in, v_mid, v_out, in_sems, out_sems,
):
    pieces = [(trunk_in, trunk, 0), (trunk_in, trunk, 1), (branch_in, branch, 0), (branch_in, branch, 1)]
    loads = [
        pltpu.make_async_copy(src.at[c], dst.at[c], in_sems.at[k])
        for k, (src, dst, c) in enumerate(pieces)
    ]
    for load in loads:
        load.start()
    stores = []

    def put(src, c, spots, held, out):
        rows = 8 * len(spots)
        for k, spot in enumerate(spots):
            tile = src[c, spot].astype(F32)
            row = c * rows + 8 * k
            held[row : row + 8, 0:128] = tile[:8]
            held[row : row + 8, 128:256] = tile[8:]
        span = pl.ds(c * rows, rows)
        store = pltpu.make_async_copy(held.at[span], out.at[span], out_sems.at[len(stores)])
        store.start()
        stores.append(store)

    for c in range(2):
        loads[c].wait()
        for k, (held, out) in enumerate(((v_in, g_v_in), (v_mid, g_v_mid), (v_out, g_v_out))):
            put(trunk, c, range(16 * k, 16 * k + 16), held, out)
    singles, doubles = tile_spots()
    for c in range(2):
        loads[2 + c].wait()
        put(branch, c, singles, w_in, g_w_in)
        put(branch, c, doubles[:16], w_mid, g_w_mid)
        put(branch, c, doubles[16:], w_out, g_w_out)
    square = jnp.sum(trunk[0, LOSS_TILE].astype(F32), keepdims=True)
    loss[...] = square * loss_scale
    for store in stores:
        store.wait()


def on_device(samples, point_index, targets, w_in, w_mid, w_out, v_in, v_mid, v_out):
    samp, pts = targets.shape
    total_cells = samp * lax.axis_size("batch") * pts * lax.axis_size("grid")
    sensors, hidden = w_in.shape
    grad_factor = 64.0 / math.sqrt(total_cells) * w_out.shape[1] ** (-0.5)
    chunks = 4
    any_spec = pl.BlockSpec(memory_space=pl.ANY)
    vmem = pl.BlockSpec(memory_space=pltpu.VMEM)
    inputs = (samples, point_index, targets, w_in, w_mid, w_out, v_in, v_mid, v_out)
    v = pltpu.VMEM
    scratch = [v(a.shape, a.dtype) for a in inputs]
    scratch += [v((hidden, pts), BF)] * 5
    scratch += [v((samp, hidden), BF)] * 3 + [v((hidden, samp), BF), v((samp, hidden), BF)]
    scratch += [v((8, 1024), F32)]
    for tiles, most in ((BRANCH_TILES, 2), (TRUNK_TILES, 1)):
        scratch += [
            v((2, tiles, *TILE), F32),
            v((tiles, *TILE), BF),
            v((tiles, *TILE), BF),
            v((tiles, *TILE), BF),
            v((most, CHIPS, *TILE), BF),
            v((most, *TILE), BF),
        ]
    scratch += [
        pltpu.SemaphoreType.DMA((8,)),
        pltpu.SemaphoreType.DMA((chunks,)),
        pltpu.SemaphoreType.DMA((2, 6)),
        pltpu.SemaphoreType.DMA((2, 6)),
    ]
    branch, trunk = pl.pallas_call(
        functools.partial(step_kernel, grad_factor),
        out_shape=(
            jax.ShapeDtypeStruct((2, BRANCH_TILES, *TILE), BF),
            jax.ShapeDtypeStruct((2, TRUNK_TILES, *TILE), BF),
        ),
        in_specs=[any_spec] * 9,
        out_specs=[any_spec] * 2,
        scratch_shapes=scratch,
        compiler_params=pltpu.CompilerParams(
            collective_id=0, has_side_effects=True, vmem_limit_bytes=58 << 20
        ),
        name="deeponet_step",
    )(*inputs)
    shapes = [(sensors, hidden)] + [(hidden, hidden)] * 5 + [(1, 1)]
    outs = pl.pallas_call(
        functools.partial(spread_kernel, 1.0 / (2.0 * total_cells)),
        out_shape=[jax.ShapeDtypeStruct(s, F32) for s in shapes],
        in_specs=[any_spec] * 2,
        out_specs=[any_spec] * 6 + [vmem],
        scratch_shapes=[v((2, BRANCH_TILES, *TILE), BF), v((2, TRUNK_TILES, *TILE), BF)]
        + [v(s, F32) for s in shapes[:6]]
        + [pltpu.SemaphoreType.DMA((4,)), pltpu.SemaphoreType.DMA((12,))],
        compiler_params=pltpu.CompilerParams(vmem_limit_bytes=60 << 20),
        name="spread_gradients",
    )(branch, trunk)
    return (*outs[:6], outs[6].reshape(()))


def solution(mesh):
    placed = (P("batch", None), P(None, "grid"), P("batch", "grid"), P(), P(), P(), P(), P(), P())
    return jax.shard_map(
        on_device,
        mesh=mesh,
        in_specs=placed,
        out_specs=(P(), P(), P(), P(), P(), P(), P()),
        check_vma=False,
    )
```

```python
import functools
import itertools
import math

import jax
import jax.numpy as jnp
from jax import lax
from jax.experimental import pallas as pl
from jax.experimental.pallas import tpu as pltpu
from jax.sharding import PartitionSpec as P

MESH = pl.DeviceIdType.MESH
BF = jnp.bfloat16
F32 = jnp.float32

GRID_SIDE = 8192
S0, S1, S2, S3, S4 = (
    6.283185160089221, -41.34165503135105, 81.60100406887733, -76.54978218664795, 39.536705209824365,
)
ROUNDER = 12582912.0

CHIPS = 64
TILE = (16, 128)
BRANCH_TILES, TRUNK_TILES, FIRST_TILES = 96, 32, 16


def dot(left, right, left_dim, right_dim):
    return lax.dot_general(
        left, right, (((left_dim,), (right_dim,)), ((), ())), preferred_element_type=F32
    )


def wave(phase):
    turn = phase - ((phase + ROUNDER) - ROUNDER)
    y = 0.25 - jnp.abs(turn)
    sq = y * y
    return y * (S0 + sq * (S1 + sq * (S2 + sq * (S3 + sq * S4))))


def waves(turns, count):
    order = lax.broadcasted_iota(jnp.int32, (8, 1), 0).astype(F32) + 1.0
    phase = order * turns
    sines, cosines = [wave(phase - 0.25)], [wave(phase)]
    while len(sines) * 8 < count:
        by_sin, by_cos = sines[-1][7:8], cosines[-1][7:8]
        pairs = list(zip(sines, cosines))
        sines += [s * by_cos + c * by_sin for s, c in pairs]
        cosines += [c * by_cos - s * by_sin for s, c in pairs]
    return jnp.concatenate(sines, axis=0), jnp.concatenate(cosines, axis=0)


def coords():
    b = lax.axis_index("batch")
    g = lax.axis_index("grid")
    return b // 2, g // 4, ((g // 2) % 2) * 2 + b % 2, g % 2


def device(x, y, z, core):
    return {"batch": x * 2 + z % 2, "grid": y * 4 + (z // 2) * 2 + core}


def remote(src, dst, sems, k, target):
    return pltpu.make_async_remote_copy(
        src_ref=src,
        dst_ref=dst,
        send_sem=sems.at[0, k],
        recv_sem=sems.at[1, k],
        device_id=target,
        device_id_type=MESH,
    )


def wait_bytes(ref, sem):
    pltpu.make_async_copy(ref, ref, sem).wait()


OFFSETS = sorted(
    itertools.product(range(4), repeat=3), key=lambda o: -sum(min(d, 4 - d) for d in o)
)


def chip_tiles(rank):
    even = (rank // 16 + rank // 4 + rank) % 2 == 0
    return 3 * (rank // 2) + (rank % 2) * (1 if even else 2), 2 if even else 1


class Chips:
    def __init__(self):
        self.x, self.y, self.z, self.core = coords()
        self.rank = (self.x * 4 + self.y) * 4 + self.z
        self.odd = (self.x + self.y + self.z) % 2
        self.sibling = device(self.x, self.y, self.z, 1 - self.core)
        xs = [(self.x + d) % 4 for d in range(4)]
        ys = [(self.y + d) % 4 for d in range(4)]
        zs = [(self.z + d) % 4 for d in range(4)]
        ranks = [x * 16 for x in xs], [y * 4 for y in ys], zs
        batches = [x * 2 for x in xs], [z % 2 for z in zs]
        grids = [y * 4 + self.core for y in ys], [(z // 2) * 2 for z in zs]
        self.all = [
            (
                sum(o),
                ranks[0][o[0]] + ranks[1][o[1]] + ranks[2][o[2]],
                {"batch": batches[0][o[0]] + batches[1][o[2]], "grid": grids[0][o[1]] + grids[1][o[2]]},
            )
            for o in OFFSETS
        ]
        self.others = self.all[:-1]


class Reducer:
    def __init__(self, chips, own, pair_send, pair_recv, send, recv, half, out, sems, counts):
        self.chips = chips
        self.own, self.pair_send, self.pair_recv = own, pair_send, pair_recv
        self.send, self.recv, self.half, self.out = send, recv, half, out
        self.sems, self.counts = sems, counts
        self.tiles = own.shape[1]
        self.readers = chips.others

    def by_parity(self, action):
        for odd in range(2):
            pl.when(self.chips.odd == odd)(functools.partial(action, odd))

    def place(self, rank, odd):
        if sum(self.counts) == 3:
            return 3 * (rank // 2) + (rank % 2) * (1 + odd)
        return rank // 2

    def start_pair(self):
        self.pair_send[...] = self.own[1 - self.chips.core].astype(BF)
        remote(self.pair_send, self.pair_recv, self.sems, 0, self.chips.sibling).start()

    def start_scatter(self):
        chips = self.chips
        wait_bytes(self.pair_recv, self.sems.at[1, 0])
        self.send[...] = (self.own[chips.core] + self.pair_recv[...].astype(F32)).astype(BF)

        def go(odd):
            for k in range(self.counts[odd]):
                self.recv[k, chips.rank] = self.send[self.place(chips.rank, odd) + k]
            for turn, rank, target in chips.others:
                theirs = (odd + turn) % 2
                count = self.counts[theirs]
                if count:
                    src = self.send.at[pl.ds(self.place(rank, theirs), count)]
                    dst = self.recv.at[pl.ds(0, count), chips.rank]
                    remote(src, dst, self.sems, 1, target).start()

        self.by_parity(go)

    def start_gather(self):
        chips = self.chips

        def go(odd):
            count = self.counts[odd]
            if not count:
                return
            wait_bytes(self.recv.at[pl.ds(0, count), pl.ds(0, CHIPS - 1)], self.sems.at[1, 1])
            spot = self.place(chips.rank, odd)
            for k in range(count):
                self.half[spot + k] = jnp.sum(self.recv[k].astype(F32), axis=0).astype(BF)
            part = self.half.at[pl.ds(spot, count)]
            for _, _, target in self.readers:
                remote(part, part, self.sems, 3, target).start()

        self.by_parity(go)

    def start_return(self):
        def go(odd):
            wait_bytes(self.pair_send.at[pl.ds(0, self.tiles - self.counts[odd])], self.sems.at[1, 3])

        self.by_parity(go)
        out = self.out.at[self.chips.core]
        remote(self.half, out, self.sems, 4, self.chips.sibling).start()
        pltpu.make_async_copy(self.half, out, self.sems.at[0, 5]).start()

    def sent(self, odd):
        count = self.counts[odd]
        wait_bytes(self.pair_send.at[pl.ds(0, self.tiles - count)], self.sems.at[0, 1])
        if count:
            wait_bytes(self.recv.at[pl.ds(0, count), pl.ds(0, CHIPS - 1)], self.sems.at[0, 3])

    def finish(self):
        wait_bytes(self.pair_send, self.sems.at[0, 0])
        self.by_parity(self.sent)
        wait_bytes(self.pair_send, self.sems.at[0, 4])
        wait_bytes(self.pair_send, self.sems.at[0, 5])
        wait_bytes(self.pair_recv, self.sems.at[1, 4])


class PlaneReducer(Reducer):
    def __init__(self, chips, *refs):
        super().__init__(chips, *refs, (1, 1))
        self.readers = [other for o, other in zip(OFFSETS, chips.others) if o[0] == 0]

    def by_parity(self, action):
        action(0)

    def place(self, rank, odd):
        return rank % 16

    def sent(self, odd):
        wait_bytes(self.recv.at[0, pl.ds(0, CHIPS - 1)], self.sems.at[0, 1])
        wait_bytes(self.recv.at[0, pl.ds(0, len(self.readers))], self.sems.at[0, 3])


class SquareReducer:
    def __init__(self, chips, own, pair, recv, total, out, sems):
        self.chips, self.own, self.pair, self.recv = chips, own, pair, recv
        self.total, self.out, self.sems = total, out, sems

    def start_pair(self):
        remote(self.own, self.pair, self.sems, 0, self.chips.sibling).start()

    def start_scatter(self):
        wait_bytes(self.pair, self.sems.at[1, 0])
        rank = self.chips.rank
        self.recv[rank] = self.own[...] + self.pair[...]
        for _, _, target in self.chips.others:
            remote(self.recv.at[rank], self.recv.at[rank], self.sems, 1, target).start()

    def start_return(self):
        wait_bytes(self.recv.at[pl.ds(0, CHIPS - 1)], self.sems.at[1, 1])
        self.total[...] = jnp.sum(self.recv[...], axis=0)
        pltpu.make_async_copy(self.total, self.out, self.sems.at[0, 2]).start()

    def finish(self):
        wait_bytes(self.own, self.sems.at[0, 0])
        wait_bytes(self.recv.at[pl.ds(0, CHIPS - 1)], self.sems.at[0, 1])
        wait_bytes(self.total, self.sems.at[0, 2])


def tile_spots():
    places = [chip_tiles(r) for r in range(CHIPS)]
    return [s for s, _ in places], [s + 1 for s, n in places if n == 2]


def step_kernel(
    grad_factor,
    samples_in, index_in, targets_in, w_in_in, w_mid_in, w_out_in, v_in_in, v_mid_in, v_out_in,
    branch_out, trunk_out, first_out, square_out,
    samples, index, targets, w_in, w_mid, w_out, v_in, v_mid, v_out,
    feats, t_one, t_two, basis, basis_grad, b_one, b_two, coeff, coeff_t, coeff_grad,
    squares,
    branch_own, branch_pair_send, branch_pair_recv, branch_send, branch_recv, branch_half,
    trunk_own, trunk_pair_send, trunk_pair_recv, trunk_send, trunk_recv, trunk_half,
    first_own, first_pair_send, first_pair_recv, first_send, first_recv, first_half,
    square_own, square_pair, square_recv, square_total,
    local_sems, target_sems, branch_sems, trunk_sems, first_sems, square_sems,
):
    samp, pts = targets.shape
    chunks = target_sems.shape[0]
    chunk = samp // chunks
    chips = Chips()
    branch = Reducer(
        chips, branch_own, branch_pair_send, branch_pair_recv, branch_send, branch_recv,
        branch_half, branch_out, branch_sems, (2, 1),
    )
    trunk = Reducer(
        chips, trunk_own, trunk_pair_send, trunk_pair_recv, trunk_send, trunk_recv,
        trunk_half, trunk_out, trunk_sems, (0, 1),
    )
    first = PlaneReducer(
        chips, first_own, first_pair_send, first_pair_recv, first_send, first_recv,
        first_half, first_out, first_sems,
    )
    square = SquareReducer(
        chips, square_own, square_pair, square_recv, square_total, square_out, square_sems
    )

    loads = []
    for k, (src, dst) in enumerate(
        (
            (index_in, index), (v_in_in, v_in), (v_mid_in, v_mid), (v_out_in, v_out),
            (w_in_in, w_in), (w_mid_in, w_mid), (w_out_in, w_out), (samples_in, samples),
        )
    ):
        copy = pltpu.make_async_copy(src, dst, local_sems.at[k])
        copy.start()
        loads.append(copy)
    target_loads = []
    for k in range(chunks):
        rows = pl.ds(k * chunk, chunk)
        copy = pltpu.make_async_copy(targets_in.at[rows], targets.at[rows], target_sems.at[k])
        copy.start()
        target_loads.append(copy)

    barrier = pltpu.get_barrier_semaphore()

    def greet(target):
        pl.semaphore_signal(barrier, inc=1, device_id=target, device_id_type=MESH)

    greet(chips.sibling)
    for _, _, target in chips.others:
        greet(target)

    for k in range(4):
        loads[k].wait()
    quarter = feats.shape[0] // 4
    v_in_t, v_mid_t, v_out_t = v_in[...].T, v_mid[...].T, v_out[...].T
    wide = 1024
    block = 512
    blocks = pts // block

    def trunk_feats(p):
        cols = pl.ds(p * block, block)
        for axis in range(2):
            turns = (2.0 * index[axis : axis + 1, cols].astype(F32) + 1.0) * (0.25 / GRID_SIDE)
            sines, cosines = waves(turns, quarter)
            base = 2 * axis * quarter
            feats[base : base + quarter, cols] = sines.astype(BF)
            feats[base + quarter : base + 2 * quarter, cols] = cosines.astype(BF)

    def trunk_one(p):
        cols = pl.ds(p * block, block)
        t_one[:, cols] = jnp.tanh(dot(v_in_t, feats[:, cols], 1, 0)).astype(BF)

    def trunk_two(p):
        cols = pl.ds(p * block, block)
        t_two[:, cols] = jnp.tanh(dot(v_mid_t, t_one[:, cols], 1, 0)).astype(BF)

    def trunk_basis(p):
        cols = pl.ds(p * block, block)
        basis[:, cols] = dot(v_out_t, t_two[:, cols], 1, 0).astype(BF)

    quarter_rows = samp // 4

    def branch_one(k):
        rows = pl.ds(k * quarter_rows, quarter_rows)
        b_one[rows, :] = jnp.tanh(dot(samples[rows, :], w_in[...], 1, 0)).astype(BF)

    def branch_two(k):
        rows = pl.ds(k * quarter_rows, quarter_rows)
        b_two[rows, :] = jnp.tanh(dot(b_one[rows, :], w_mid[...], 1, 0)).astype(BF)

    def branch_coeff(k):
        rows = pl.ds(k * quarter_rows, quarter_rows)
        coeff[rows, :] = dot(b_two[rows, :], w_out[...], 1, 0).astype(BF)

    stages = (trunk_feats, trunk_one, trunk_two, trunk_basis)
    branch_stages = (branch_one, branch_two, branch_coeff)
    branch_from = 5
    for step in range(blocks + len(stages) - 1):
        if step == branch_from:
            for k in range(4, 8):
                loads[k].wait()
        for lag, stage in enumerate(stages):
            if 0 <= step - lag < blocks:
                stage(step - lag)
        for lag, stage in enumerate(branch_stages):
            if 0 <= step - branch_from - lag < 4:
                stage(step - branch_from - lag)
    coeff_t[...] = coeff[...].T

    squares[...] = jnp.zeros_like(squares)
    for k in range(chunks):
        rows = pl.ds(k * chunk, chunk)
        target_loads[k].wait()
        scaled = coeff[rows, :] * jnp.asarray(1.0 / 16.0, BF)
        for p in range(0, pts, wide):
            cols = pl.ds(p, wide)
            residual = dot(scaled, basis[:, cols], 1, 0) - targets[rows, cols].astype(F32)
            targets[rows, cols] = (residual * grad_factor).astype(BF)
            squared = residual * residual
            squares[...] += jnp.sum(squared.reshape(chunk // 8, 8, wide), axis=0)
        coeff_grad[rows, :] = dot(targets[rows, :], basis[...], 1, 1).astype(BF)

    grad = coeff_grad[...]
    part_out = dot(b_two[...], grad, 0, 0)
    slope = 1.0 - jnp.square(b_two[...].astype(F32))
    back_two = (dot(grad, w_out[...], 1, 1) * slope).astype(BF)
    part_mid = dot(b_one[...], back_two, 0, 0)
    slope = 1.0 - jnp.square(b_one[...].astype(F32))
    back_one = (dot(back_two, w_mid[...], 1, 1) * slope).astype(BF)
    part_in = dot(samples[...], back_one, 0, 0)
    square_own[...] = jnp.sum(jnp.sum(squares[...].reshape(8, wide // 128, 128), axis=1), axis=0, keepdims=True)

    def pack(own, part, core, spots, row):
        for k, spot in enumerate(spots):
            strip = part[row + 8 * k : row + 8 * k + 8]
            own[core, spot, 0:8] = strip[:, :128]
            own[core, spot, 8:16] = strip[:, 128:]

    singles, doubles = tile_spots()
    for c in range(2):
        pack(branch_own, part_in, c, singles, c * 512)
        pack(branch_own, part_mid, c, doubles[:16], c * 128)
        pack(branch_own, part_out, c, doubles[16:], c * 128)

    pl.semaphore_wait(barrier, CHIPS)
    branch.start_pair()
    square.start_pair()

    for p in range(0, pts, wide):
        cols = pl.ds(p, wide)
        basis_grad[:, cols] = dot(coeff_t[...], targets[:, cols], 1, 0).astype(BF)
        if p == wide:
            branch.start_scatter()
            square.start_scatter()

    def pack_trunk(own, part, spot):
        for c in range(2):
            pack(own, part, c, range(spot, spot + 16), c * 128)

    def back(weight, grad, hidden, result):
        for p in range(0, pts, wide):
            cols = pl.ds(p, wide)
            slope = 1.0 - jnp.square(hidden[:, cols].astype(F32))
            result[:, cols] = (dot(weight[...], grad[:, cols], 1, 0) * slope).astype(BF)

    back_two_t, back_one_t = basis, basis_grad
    pack_trunk(trunk_own, dot(t_two[...], basis_grad[...], 1, 1), 0)
    back(v_out, basis_grad, t_two, back_two_t)
    pack_trunk(trunk_own, dot(t_one[...], back_two_t[...], 1, 1), 16)
    trunk.start_pair()
    back(v_mid, back_two_t, t_one, back_one_t)
    trunk.start_scatter()
    pack_trunk(first_own, dot(feats[...], back_one_t[...], 1, 1), 0)
    first.start_pair()
    first.start_scatter()

    branch.start_gather()
    trunk.start_gather()
    square.start_return()
    first.start_gather()
    branch.start_return()
    trunk.start_return()
    first.start_return()
    trunk.finish()
    branch.finish()
    first.finish()
    square.finish()


def spread_kernel(
    loss_scale, branch_in, trunk_in, first_in, square_in, g_w_in, g_w_mid, g_w_out, g_v_in, g_v_mid, g_v_out, loss_out,
    branch, trunk, first, square, loss, w_in, w_mid, w_out, v_in, v_mid, v_out, in_sems, out_sems,
):
    loads = [
        pltpu.make_async_copy(src, dst, in_sems.at[k])
        for k, (src, dst) in enumerate(
            (
                (branch_in.at[0], branch.at[0]), (branch_in.at[1], branch.at[1]),
                (trunk_in, trunk), (first_in, first), (square_in, square),
            )
        )
    ]
    for load in loads:
        load.start()
    stores = []

    def put(src, c, spots, held, out):
        rows = 8 * len(spots)
        for k, spot in enumerate(spots):
            tile = src[c, spot].astype(F32)
            row = c * rows + 8 * k
            held[row : row + 8, 0:128] = tile[:8]
            held[row : row + 8, 128:256] = tile[8:]
        span = pl.ds(c * rows, rows)
        store = pltpu.make_async_copy(held.at[span], out.at[span], out_sems.at[len(stores)])
        store.start()
        stores.append(store)

    singles, doubles = tile_spots()
    for c in range(2):
        loads[c].wait()
        put(branch, c, singles, w_in, g_w_in)
        put(branch, c, doubles[:16], w_mid, g_w_mid)
        put(branch, c, doubles[16:], w_out, g_w_out)
    loads[2].wait()
    loads[3].wait()
    for c in range(2):
        put(trunk, c, range(16), v_out, g_v_out)
        put(trunk, c, range(16, 32), v_mid, g_v_mid)
        put(first, c, range(16), v_in, g_v_in)
    loads[4].wait()
    loss[...] = jnp.sum(square[...], keepdims=True) * loss_scale
    stores.append(pltpu.make_async_copy(loss, loss_out, out_sems.at[len(stores)]))
    stores[-1].start()
    for store in stores:
        store.wait()


def on_device(samples, point_index, targets, w_in, w_mid, w_out, v_in, v_mid, v_out):
    samp, pts = targets.shape
    total_cells = samp * lax.axis_size("batch") * pts * lax.axis_size("grid")
    sensors, hidden = w_in.shape
    grad_factor = 64.0 / math.sqrt(total_cells) * w_out.shape[1] ** (-0.5)
    chunks = 4
    any_spec = pl.BlockSpec(memory_space=pl.ANY)
    inputs = (samples, point_index, targets, w_in, w_mid, w_out, v_in, v_mid, v_out)
    v = pltpu.VMEM
    scratch = [v(a.shape, a.dtype) for a in inputs]
    scratch += [v((hidden, pts), BF)] * 5
    scratch += [v((samp, hidden), BF)] * 3 + [v((hidden, samp), BF), v((samp, hidden), BF)]
    scratch += [v((8, 1024), F32)]
    for tiles, most in ((BRANCH_TILES, 2), (TRUNK_TILES, 1), (FIRST_TILES, 1)):
        scratch += [
            v((2, tiles, *TILE), F32),
            v((tiles, *TILE), BF),
            v((tiles, *TILE), BF),
            v((tiles, *TILE), BF),
            v((most, CHIPS, *TILE), BF),
            v((tiles, *TILE), BF),
        ]
    scratch += [v((1, 128), F32), v((1, 128), F32), v((CHIPS, 1, 128), F32), v((1, 128), F32)]
    scratch += [
        pltpu.SemaphoreType.DMA((8,)),
        pltpu.SemaphoreType.DMA((chunks,)),
        pltpu.SemaphoreType.DMA((2, 6)),
        pltpu.SemaphoreType.DMA((2, 6)),
        pltpu.SemaphoreType.DMA((2, 6)),
        pltpu.SemaphoreType.DMA((2, 3)),
    ]
    branch, trunk, first, square = pl.pallas_call(
        functools.partial(step_kernel, grad_factor),
        out_shape=(
            jax.ShapeDtypeStruct((2, BRANCH_TILES, *TILE), BF),
            jax.ShapeDtypeStruct((2, TRUNK_TILES, *TILE), BF),
            jax.ShapeDtypeStruct((2, FIRST_TILES, *TILE), BF),
            jax.ShapeDtypeStruct((1, 128), F32),
        ),
        in_specs=[any_spec] * 9,
        out_specs=[any_spec] * 4,
        scratch_shapes=scratch,
        compiler_params=pltpu.CompilerParams(
            collective_id=0, has_side_effects=True, vmem_limit_bytes=58 << 20
        ),
        name="deeponet_step",
    )(*inputs)
    shapes = [(sensors, hidden)] + [(hidden, hidden)] * 5 + [(1, 1)]
    outs = pl.pallas_call(
        functools.partial(spread_kernel, 1.0 / (2.0 * total_cells)),
        out_shape=[jax.ShapeDtypeStruct(s, F32) for s in shapes],
        in_specs=[any_spec] * 4,
        out_specs=[any_spec] * 7,
        scratch_shapes=[v((2, n, *TILE), BF) for n in (BRANCH_TILES, TRUNK_TILES, FIRST_TILES)]
        + [v((1, 128), F32), v((1, 1), F32)]
        + [v(s, F32) for s in shapes[:6]]
        + [pltpu.SemaphoreType.DMA((5,)), pltpu.SemaphoreType.DMA((13,))],
        compiler_params=pltpu.CompilerParams(vmem_limit_bytes=60 << 20),
        name="spread_gradients",
    )(branch, trunk, first, square)
    return (*outs[:6], outs[6].reshape(()))


def solution(mesh):
    placed = (P("batch", None), P(None, "grid"), P("batch", "grid"), P(), P(), P(), P(), P(), P())
    return jax.shard_map(
        on_device,
        mesh=mesh,
        in_specs=placed,
        out_specs=(P(), P(), P(), P(), P(), P(), P()),
        check_vma=False,
    )
```

```python
import functools
import itertools
import math

import jax
import jax.numpy as jnp
from jax import lax
from jax.experimental import pallas as pl
from jax.experimental.pallas import tpu as pltpu
from jax.sharding import PartitionSpec as P

MESH = pl.DeviceIdType.MESH
BF = jnp.bfloat16
F32 = jnp.float32

GRID_SIDE = 8192
S0, S1, S2, S3, S4 = (
    6.283185160089221, -41.34165503135105, 81.60100406887733, -76.54978218664795, 39.536705209824365,
)
ROUNDER = 12582912.0

CHIPS = 64
TILE = (16, 128)
BRANCH_TILES, TRUNK_TILES, FIRST_TILES = 96, 32, 16


def dot(left, right, left_dim, right_dim):
    return lax.dot_general(
        left, right, (((left_dim,), (right_dim,)), ((), ())), preferred_element_type=F32
    )


def wave(phase):
    turn = phase - ((phase + ROUNDER) - ROUNDER)
    y = 0.25 - jnp.abs(turn)
    sq = y * y
    return y * (S0 + sq * (S1 + sq * (S2 + sq * (S3 + sq * S4))))


def waves(turns, count):
    order = lax.broadcasted_iota(jnp.int32, (8, 1), 0).astype(F32) + 1.0
    phase = order * turns
    sines, cosines = [wave(phase - 0.25)], [wave(phase)]
    while len(sines) * 8 < count:
        by_sin, by_cos = sines[-1][7:8], cosines[-1][7:8]
        pairs = list(zip(sines, cosines))
        sines += [s * by_cos + c * by_sin for s, c in pairs]
        cosines += [c * by_cos - s * by_sin for s, c in pairs]
    return jnp.concatenate(sines, axis=0), jnp.concatenate(cosines, axis=0)


def coords():
    b = lax.axis_index("batch")
    g = lax.axis_index("grid")
    return b // 2, g // 4, ((g // 2) % 2) * 2 + b % 2, g % 2


def device(x, y, z, core):
    return {"batch": x * 2 + z % 2, "grid": y * 4 + (z // 2) * 2 + core}


def remote(src, dst, sems, k, target):
    return pltpu.make_async_remote_copy(
        src_ref=src,
        dst_ref=dst,
        send_sem=sems.at[0, k],
        recv_sem=sems.at[1, k],
        device_id=target,
        device_id_type=MESH,
    )


def wait_bytes(ref, sem):
    pltpu.make_async_copy(ref, ref, sem).wait()


OFFSETS = sorted(
    itertools.product(range(4), repeat=3), key=lambda o: -sum(min(d, 4 - d) for d in o)
)


class Chips:
    def __init__(self):
        self.x, self.y, self.z, self.core = coords()
        self.rank = (self.x * 4 + self.y) * 4 + self.z
        self.odd = (self.x + self.y + self.z) % 2
        self.sibling = device(self.x, self.y, self.z, 1 - self.core)
        xs = [(self.x + d) % 4 for d in range(4)]
        ys = [(self.y + d) % 4 for d in range(4)]
        zs = [(self.z + d) % 4 for d in range(4)]
        ranks = [x * 16 for x in xs], [y * 4 for y in ys], zs
        batches = [x * 2 for x in xs], [z % 2 for z in zs]
        grids = [y * 4 + self.core for y in ys], [(z // 2) * 2 for z in zs]
        self.all = [
            (
                sum(o),
                (xs[o[0]], ys[o[1]], zs[o[2]]),
                ranks[0][o[0]] + ranks[1][o[1]] + ranks[2][o[2]],
                {"batch": batches[0][o[0]] + batches[1][o[2]], "grid": grids[0][o[1]] + grids[1][o[2]]},
            )
            for o in OFFSETS
        ]
        self.others = self.all[:-1]
        self.place = (self.x, self.y, self.z)


class Reducer:
    def __init__(self, chips, own, pair_send, pair_recv, send, recv, half, out, sems, counts):
        self.chips = chips
        self.own, self.pair_send, self.pair_recv = own, pair_send, pair_recv
        self.send, self.recv, self.half, self.out = send, recv, half, out
        self.sems, self.counts = sems, counts
        self.tiles = own.shape[1]
        self.readers = chips.others

    def by_parity(self, action):
        for odd in range(2):
            pl.when(self.chips.odd == odd)(functools.partial(action, odd))

    def place(self, rank, odd):
        return rank // 2

    def start_pair(self):
        self.pair_send[...] = self.own[1 - self.chips.core].astype(BF)
        remote(self.pair_send, self.pair_recv, self.sems, 0, self.chips.sibling).start()

    def start_scatter(self):
        chips = self.chips
        wait_bytes(self.pair_recv, self.sems.at[1, 0])
        self.send[...] = (self.own[chips.core] + self.pair_recv[...].astype(F32)).astype(BF)

        def go(odd):
            for k in range(self.counts[odd]):
                self.recv[k, chips.rank] = self.send[self.place(chips.rank, odd) + k]
            for turn, _, rank, target in chips.others:
                theirs = (odd + turn) % 2
                count = self.counts[theirs]
                if count:
                    src = self.send.at[pl.ds(self.place(rank, theirs), count)]
                    dst = self.recv.at[pl.ds(0, count), chips.rank]
                    remote(src, dst, self.sems, 1, target).start()

        self.by_parity(go)

    def start_gather(self):
        chips = self.chips

        def go(odd):
            count = self.counts[odd]
            if not count:
                return
            wait_bytes(self.recv.at[pl.ds(0, count), pl.ds(0, CHIPS - 1)], self.sems.at[1, 1])
            spot = self.place(chips.rank, odd)
            for k in range(count):
                self.half[spot + k] = jnp.sum(self.recv[k].astype(F32), axis=0).astype(BF)
            part = self.half.at[pl.ds(spot, count)]
            for *_, target in self.readers:
                remote(part, part, self.sems, 3, target).start()

        self.by_parity(go)

    def start_return(self):
        def go(odd):
            wait_bytes(self.pair_send.at[pl.ds(0, self.tiles - self.counts[odd])], self.sems.at[1, 3])

        self.by_parity(go)
        out = self.out.at[self.chips.core]
        remote(self.half, out, self.sems, 4, self.chips.sibling).start()
        pltpu.make_async_copy(self.half, out, self.sems.at[0, 5]).start()

    def sent(self, odd):
        count = self.counts[odd]
        wait_bytes(self.pair_send.at[pl.ds(0, self.tiles - count)], self.sems.at[0, 1])
        if count:
            wait_bytes(self.recv.at[pl.ds(0, count), pl.ds(0, CHIPS - 1)], self.sems.at[0, 3])

    def finish(self):
        wait_bytes(self.pair_send, self.sems.at[0, 0])
        self.by_parity(self.sent)
        wait_bytes(self.pair_send, self.sems.at[0, 4])
        wait_bytes(self.pair_send, self.sems.at[0, 5])
        wait_bytes(self.pair_recv, self.sems.at[1, 4])


CLASSES = ((0, 2), (1,))


def class_spot(place, axis):
    u, v = (c for k, c in enumerate(place) if k != axis)
    return 32 * axis + 8 * place[axis] + (u * 4 + v) // 2


class BranchReducer(Reducer):
    def start_scatter(self):
        chips = self.chips
        wait_bytes(self.pair_recv, self.sems.at[1, 0])
        self.send[...] = (self.own[chips.core] + self.pair_recv[...].astype(F32)).astype(BF)

        def go(odd):
            for k, axis in enumerate(CLASSES[odd]):
                self.recv[k, chips.rank] = self.send[class_spot(chips.place, axis)]
            for turn, place, _, target in chips.others:
                for k, axis in enumerate(CLASSES[(odd + turn) % 2]):
                    src, dst = self.send.at[class_spot(place, axis)], self.recv.at[k, chips.rank]
                    remote(src, dst, self.sems, 1, target).start()

        self.by_parity(go)

    def start_gather(self):
        chips = self.chips

        def go(odd):
            count = self.counts[odd]
            wait_bytes(self.recv.at[pl.ds(0, count), pl.ds(0, CHIPS - 1)], self.sems.at[1, 1])
            for k, axis in enumerate(CLASSES[odd]):
                spot = class_spot(chips.place, axis)
                self.half[spot] = jnp.sum(self.recv[k].astype(F32), axis=0).astype(BF)
                part = self.half.at[spot]
                for o, (*_, target) in zip(OFFSETS, chips.others):
                    if o[axis] == 0:
                        remote(part, part, self.sems, 3, target).start()

        self.by_parity(go)

    def start_line(self):
        def go(odd):
            wait_bytes(self.pair_send.at[pl.ds(0, 24 - self.counts[odd])], self.sems.at[1, 3])

        self.by_parity(go)
        for o, (*_, target) in zip(OFFSETS, self.chips.others):
            if o.count(0) == 2:
                axis = next(k for k in range(3) if o[k])
                part = self.half.at[pl.ds(32 * axis + 8 * self.chips.place[axis], 8)]
                remote(part, part, self.sems, 6, target).start()

    def start_return(self):
        wait_bytes(self.pair_send.at[pl.ds(0, 72)], self.sems.at[1, 6])
        out = self.out.at[self.chips.core]
        remote(self.half, out, self.sems, 4, self.chips.sibling).start()
        pltpu.make_async_copy(self.half, out, self.sems.at[0, 5]).start()

    def sent(self, odd):
        count = self.counts[odd]
        wait_bytes(self.pair_send.at[pl.ds(0, self.tiles - count)], self.sems.at[0, 1])
        wait_bytes(self.recv.at[pl.ds(0, count), pl.ds(0, 15)], self.sems.at[0, 3])
        wait_bytes(self.pair_send.at[pl.ds(0, 72)], self.sems.at[0, 6])


class PlaneReducer(Reducer):
    def __init__(self, chips, *refs):
        super().__init__(chips, *refs, (1, 1))
        self.readers = [other for o, other in zip(OFFSETS, chips.others) if o[0] == 0]

    def by_parity(self, action):
        action(0)

    def place(self, rank, odd):
        return rank % 16

    def sent(self, odd):
        wait_bytes(self.recv.at[0, pl.ds(0, CHIPS - 1)], self.sems.at[0, 1])
        wait_bytes(self.recv.at[0, pl.ds(0, len(self.readers))], self.sems.at[0, 3])


class SquareReducer:
    def __init__(self, chips, own, pair, recv, total, out, sems):
        self.chips, self.own, self.pair, self.recv = chips, own, pair, recv
        self.total, self.out, self.sems = total, out, sems

    def start_pair(self):
        remote(self.own, self.pair, self.sems, 0, self.chips.sibling).start()

    def start_scatter(self):
        wait_bytes(self.pair, self.sems.at[1, 0])
        rank = self.chips.rank
        self.recv[rank] = self.own[...] + self.pair[...]
        for *_, target in self.chips.others:
            remote(self.recv.at[rank], self.recv.at[rank], self.sems, 1, target).start()

    def start_return(self):
        wait_bytes(self.recv.at[pl.ds(0, CHIPS - 1)], self.sems.at[1, 1])
        self.total[...] = jnp.sum(self.recv[...], axis=0)
        pltpu.make_async_copy(self.total, self.out, self.sems.at[0, 2]).start()

    def finish(self):
        wait_bytes(self.own, self.sems.at[0, 0])
        wait_bytes(self.recv.at[pl.ds(0, CHIPS - 1)], self.sems.at[0, 1])
        wait_bytes(self.total, self.sems.at[0, 2])


def tile_spots():
    singles, doubles = [], []
    for place in itertools.product(range(4), repeat=3):
        axes = CLASSES[sum(place) % 2]
        singles.append(class_spot(place, axes[0]))
        doubles += [class_spot(place, axis) for axis in axes[1:]]
    return singles, doubles


def step_kernel(
    grad_factor,
    samples_in, index_in, targets_in, w_in_in, w_mid_in, w_out_in, v_in_in, v_mid_in, v_out_in,
    branch_out, trunk_out, first_out, square_out,
    samples, index, targets, w_in, w_mid, w_out, v_in, v_mid, v_out,
    feats, t_one, t_two, basis, basis_grad, b_one, b_two, coeff, coeff_t, coeff_grad,
    squares,
    branch_own, branch_pair_send, branch_pair_recv, branch_send, branch_recv, branch_half,
    trunk_own, trunk_pair_send, trunk_pair_recv, trunk_send, trunk_recv, trunk_half,
    first_own, first_pair_send, first_pair_recv, first_send, first_recv, first_half,
    square_own, square_pair, square_recv, square_total,
    local_sems, target_sems, branch_sems, trunk_sems, first_sems, square_sems,
):
    samp, pts = targets.shape
    chunks = target_sems.shape[0]
    chunk = samp // chunks
    chips = Chips()
    branch = BranchReducer(
        chips, branch_own, branch_pair_send, branch_pair_recv, branch_send, branch_recv,
        branch_half, branch_out, branch_sems, (2, 1),
    )
    trunk = Reducer(
        chips, trunk_own, trunk_pair_send, trunk_pair_recv, trunk_send, trunk_recv,
        trunk_half, trunk_out, trunk_sems, (0, 1),
    )
    first = PlaneReducer(
        chips, first_own, first_pair_send, first_pair_recv, first_send, first_recv,
        first_half, first_out, first_sems,
    )
    square = SquareReducer(
        chips, square_own, square_pair, square_recv, square_total, square_out, square_sems
    )

    loads = []
    for k, (src, dst) in enumerate(
        (
            (index_in, index), (v_in_in, v_in), (v_mid_in, v_mid), (v_out_in, v_out),
            (w_in_in, w_in), (w_mid_in, w_mid), (w_out_in, w_out), (samples_in, samples),
        )
    ):
        copy = pltpu.make_async_copy(src, dst, local_sems.at[k])
        copy.start()
        loads.append(copy)
    target_loads = []
    for k in range(chunks):
        rows = pl.ds(k * chunk, chunk)
        copy = pltpu.make_async_copy(targets_in.at[rows], targets.at[rows], target_sems.at[k])
        copy.start()
        target_loads.append(copy)

    barrier = pltpu.get_barrier_semaphore()

    def greet(target):
        pl.semaphore_signal(barrier, inc=1, device_id=target, device_id_type=MESH)

    greet(chips.sibling)
    for *_, target in chips.others:
        greet(target)

    for k in range(4):
        loads[k].wait()
    quarter = feats.shape[0] // 4
    v_in_t, v_mid_t, v_out_t = v_in[...].T, v_mid[...].T, v_out[...].T
    wide = 1024
    block = 512
    blocks = pts // block

    def trunk_feats(p):
        cols = pl.ds(p * block, block)
        for axis in range(2):
            turns = (2.0 * index[axis : axis + 1, cols].astype(F32) + 1.0) * (0.25 / GRID_SIDE)
            sines, cosines = waves(turns, quarter)
            base = 2 * axis * quarter
            feats[base : base + quarter, cols] = sines.astype(BF)
            feats[base + quarter : base + 2 * quarter, cols] = cosines.astype(BF)

    def trunk_one(p):
        cols = pl.ds(p * block, block)
        t_one[:, cols] = jnp.tanh(dot(v_in_t, feats[:, cols], 1, 0)).astype(BF)

    def trunk_two(p):
        cols = pl.ds(p * block, block)
        t_two[:, cols] = jnp.tanh(dot(v_mid_t, t_one[:, cols], 1, 0)).astype(BF)

    def trunk_basis(p):
        cols = pl.ds(p * block, block)
        basis[:, cols] = dot(v_out_t, t_two[:, cols], 1, 0).astype(BF)

    quarter_rows = samp // 4

    def branch_one(k):
        rows = pl.ds(k * quarter_rows, quarter_rows)
        b_one[rows, :] = jnp.tanh(dot(samples[rows, :], w_in[...], 1, 0)).astype(BF)

    def branch_two(k):
        rows = pl.ds(k * quarter_rows, quarter_rows)
        b_two[rows, :] = jnp.tanh(dot(b_one[rows, :], w_mid[...], 1, 0)).astype(BF)

    def branch_coeff(k):
        rows = pl.ds(k * quarter_rows, quarter_rows)
        coeff[rows, :] = dot(b_two[rows, :], w_out[...], 1, 0).astype(BF)

    stages = (trunk_feats, trunk_one, trunk_two, trunk_basis)
    branch_stages = (branch_one, branch_two, branch_coeff)
    branch_from = 5
    for step in range(blocks + len(stages) - 1):
        if step == branch_from:
            for k in range(4, 8):
                loads[k].wait()
        for lag, stage in enumerate(stages):
            if 0 <= step - lag < blocks:
                stage(step - lag)
        for lag, stage in enumerate(branch_stages):
            if 0 <= step - branch_from - lag < 4:
                stage(step - branch_from - lag)
    coeff_t[...] = coeff[...].T

    squares[...] = jnp.zeros_like(squares)
    for k in range(chunks):
        rows = pl.ds(k * chunk, chunk)
        target_loads[k].wait()
        scaled = coeff[rows, :] * jnp.asarray(1.0 / 16.0, BF)
        for p in range(0, pts, wide):
            cols = pl.ds(p, wide)
            residual = dot(scaled, basis[:, cols], 1, 0) - targets[rows, cols].astype(F32)
            targets[rows, cols] = (residual * grad_factor).astype(BF)
            squared = residual * residual
            squares[...] += jnp.sum(squared.reshape(chunk // 8, 8, wide), axis=0)
        coeff_grad[rows, :] = dot(targets[rows, :], basis[...], 1, 1).astype(BF)

    grad = coeff_grad[...]
    part_out = dot(b_two[...], grad, 0, 0)
    slope = 1.0 - jnp.square(b_two[...].astype(F32))
    back_two = (dot(grad, w_out[...], 1, 1) * slope).astype(BF)
    part_mid = dot(b_one[...], back_two, 0, 0)
    slope = 1.0 - jnp.square(b_one[...].astype(F32))
    back_one = (dot(back_two, w_mid[...], 1, 1) * slope).astype(BF)
    part_in = dot(samples[...], back_one, 0, 0)
    square_own[...] = jnp.sum(jnp.sum(squares[...].reshape(8, wide // 128, 128), axis=1), axis=0, keepdims=True)

    def pack(own, part, core, spots, row):
        for k, spot in enumerate(spots):
            strip = part[row + 8 * k : row + 8 * k + 8]
            own[core, spot, 0:8] = strip[:, :128]
            own[core, spot, 8:16] = strip[:, 128:]

    singles, doubles = tile_spots()
    for c in range(2):
        pack(branch_own, part_in, c, singles, c * 512)
        pack(branch_own, part_mid, c, doubles[:16], c * 128)
        pack(branch_own, part_out, c, doubles[16:], c * 128)

    pl.semaphore_wait(barrier, CHIPS)
    branch.start_pair()
    square.start_pair()

    for p in range(0, pts, wide):
        cols = pl.ds(p, wide)
        basis_grad[:, cols] = dot(coeff_t[...], targets[:, cols], 1, 0).astype(BF)
        if p == wide:
            branch.start_scatter()
            square.start_scatter()

    def pack_trunk(own, part, spot):
        for c in range(2):
            pack(own, part, c, range(spot, spot + 16), c * 128)

    def back(weight, grad, hidden, result):
        for p in range(0, pts, wide):
            cols = pl.ds(p, wide)
            slope = 1.0 - jnp.square(hidden[:, cols].astype(F32))
            result[:, cols] = (dot(weight[...], grad[:, cols], 1, 0) * slope).astype(BF)

    back_two_t, back_one_t = basis, basis_grad
    pack_trunk(trunk_own, dot(t_two[...], basis_grad[...], 1, 1), 0)
    back(v_out, basis_grad, t_two, back_two_t)
    pack_trunk(trunk_own, dot(t_one[...], back_two_t[...], 1, 1), 16)
    trunk.start_pair()
    back(v_mid, back_two_t, t_one, back_one_t)
    trunk.start_scatter()
    pack_trunk(first_own, dot(feats[...], back_one_t[...], 1, 1), 0)
    first.start_pair()
    first.start_scatter()

    branch.start_gather()
    trunk.start_gather()
    square.start_return()
    first.start_gather()
    branch.start_line()
    trunk.start_return()
    first.start_return()
    branch.start_return()
    trunk.finish()
    branch.finish()
    first.finish()
    square.finish()


def spread_kernel(
    loss_scale, branch_in, trunk_in, first_in, square_in, g_w_in, g_w_mid, g_w_out, g_v_in, g_v_mid, g_v_out, loss_out,
    branch, trunk, first, square, loss, w_in, w_mid, w_out, v_in, v_mid, v_out, in_sems, out_sems,
):
    loads = [
        pltpu.make_async_copy(src, dst, in_sems.at[k])
        for k, (src, dst) in enumerate(
            (
                (branch_in.at[0], branch.at[0]), (branch_in.at[1], branch.at[1]),
                (trunk_in, trunk), (first_in, first), (square_in, square),
            )
        )
    ]
    for load in loads:
        load.start()
    stores = []

    def put(src, c, spots, held, out):
        rows = 8 * len(spots)
        for k, spot in enumerate(spots):
            tile = src[c, spot].astype(F32)
            row = c * rows + 8 * k
            held[row : row + 8, 0:128] = tile[:8]
            held[row : row + 8, 128:256] = tile[8:]
        span = pl.ds(c * rows, rows)
        store = pltpu.make_async_copy(held.at[span], out.at[span], out_sems.at[len(stores)])
        store.start()
        stores.append(store)

    singles, doubles = tile_spots()
    for c in range(2):
        loads[c].wait()
        put(branch, c, singles, w_in, g_w_in)
        put(branch, c, doubles[:16], w_mid, g_w_mid)
        put(branch, c, doubles[16:], w_out, g_w_out)
    loads[2].wait()
    loads[3].wait()
    for c in range(2):
        put(trunk, c, range(16), v_out, g_v_out)
        put(trunk, c, range(16, 32), v_mid, g_v_mid)
        put(first, c, range(16), v_in, g_v_in)
    loads[4].wait()
    loss[...] = jnp.sum(square[...], keepdims=True) * loss_scale
    stores.append(pltpu.make_async_copy(loss, loss_out, out_sems.at[len(stores)]))
    stores[-1].start()
    for store in stores:
        store.wait()


def on_device(samples, point_index, targets, w_in, w_mid, w_out, v_in, v_mid, v_out):
    samp, pts = targets.shape
    total_cells = samp * lax.axis_size("batch") * pts * lax.axis_size("grid")
    sensors, hidden = w_in.shape
    grad_factor = 64.0 / math.sqrt(total_cells) * w_out.shape[1] ** (-0.5)
    chunks = 2
    any_spec = pl.BlockSpec(memory_space=pl.ANY)
    inputs = (samples, point_index, targets, w_in, w_mid, w_out, v_in, v_mid, v_out)
    v = pltpu.VMEM
    scratch = [v(a.shape, a.dtype) for a in inputs]
    scratch += [v((hidden, pts), BF)] * 5
    scratch += [v((samp, hidden), BF)] * 3 + [v((hidden, samp), BF), v((samp, hidden), BF)]
    scratch += [v((8, 1024), F32)]
    for tiles, most in ((BRANCH_TILES, 2), (TRUNK_TILES, 1), (FIRST_TILES, 1)):
        scratch += [
            v((2, tiles, *TILE), F32),
            v((tiles, *TILE), BF),
            v((tiles, *TILE), BF),
            v((tiles, *TILE), BF),
            v((most, CHIPS, *TILE), BF),
            v((tiles, *TILE), BF),
        ]
    scratch += [v((1, 128), F32), v((1, 128), F32), v((CHIPS, 1, 128), F32), v((1, 128), F32)]
    scratch += [
        pltpu.SemaphoreType.DMA((8,)),
        pltpu.SemaphoreType.DMA((chunks,)),
        pltpu.SemaphoreType.DMA((2, 7)),
        pltpu.SemaphoreType.DMA((2, 6)),
        pltpu.SemaphoreType.DMA((2, 6)),
        pltpu.SemaphoreType.DMA((2, 3)),
    ]
    branch, trunk, first, square = pl.pallas_call(
        functools.partial(step_kernel, grad_factor),
        out_shape=(
            jax.ShapeDtypeStruct((2, BRANCH_TILES, *TILE), BF),
            jax.ShapeDtypeStruct((2, TRUNK_TILES, *TILE), BF),
            jax.ShapeDtypeStruct((2, FIRST_TILES, *TILE), BF),
            jax.ShapeDtypeStruct((1, 128), F32),
        ),
        in_specs=[any_spec] * 9,
        out_specs=[any_spec] * 4,
        scratch_shapes=scratch,
        compiler_params=pltpu.CompilerParams(
            collective_id=0, has_side_effects=True, vmem_limit_bytes=58 << 20
        ),
        name="deeponet_step",
    )(*inputs)
    shapes = [(sensors, hidden)] + [(hidden, hidden)] * 5 + [(1, 1)]
    outs = pl.pallas_call(
        functools.partial(spread_kernel, 1.0 / (2.0 * total_cells)),
        out_shape=[jax.ShapeDtypeStruct(s, F32) for s in shapes],
        in_specs=[any_spec] * 4,
        out_specs=[any_spec] * 7,
        scratch_shapes=[v((2, n, *TILE), BF) for n in (BRANCH_TILES, TRUNK_TILES, FIRST_TILES)]
        + [v((1, 128), F32), v((1, 1), F32)]
        + [v(s, F32) for s in shapes[:6]]
        + [pltpu.SemaphoreType.DMA((5,)), pltpu.SemaphoreType.DMA((13,))],
        compiler_params=pltpu.CompilerParams(vmem_limit_bytes=60 << 20),
        name="spread_gradients",
    )(branch, trunk, first, square)
    return (*outs[:6], outs[6].reshape(()))


def solution(mesh):
    placed = (P("batch", None), P(None, "grid"), P("batch", "grid"), P(), P(), P(), P(), P(), P())
    return jax.shard_map(
        on_device,
        mesh=mesh,
        in_specs=placed,
        out_specs=(P(), P(), P(), P(), P(), P(), P()),
        check_vma=False,
    )
```

```python
import functools
import itertools
import math

import jax
import jax.numpy as jnp
from jax import lax
from jax.experimental import pallas as pl
from jax.experimental.pallas import tpu as pltpu
from jax.sharding import PartitionSpec as P

MESH = pl.DeviceIdType.MESH
BF = jnp.bfloat16
F32 = jnp.float32

GRID_SIDE = 8192
S0, S1, S2, S3, S4 = (
    6.283185160089221, -41.34165503135105, 81.60100406887733, -76.54978218664795, 39.536705209824365,
)
ROUNDER = 12582912.0

CHIPS = 64
TILE = (16, 128)
BRANCH_TILES, TRUNK_TILES, FIRST_TILES = 96, 32, 16


def dot(left, right, left_dim, right_dim):
    return lax.dot_general(
        left, right, (((left_dim,), (right_dim,)), ((), ())), preferred_element_type=F32
    )


def wave(phase):
    turn = phase - ((phase + ROUNDER) - ROUNDER)
    y = 0.25 - jnp.abs(turn)
    sq = y * y
    return y * (S0 + sq * (S1 + sq * (S2 + sq * (S3 + sq * S4))))


def waves(turns, count):
    order = lax.broadcasted_iota(jnp.int32, (8, 1), 0).astype(F32) + 1.0
    phase = order * turns
    sines, cosines = [wave(phase - 0.25)], [wave(phase)]
    while len(sines) * 8 < count:
        by_sin, by_cos = sines[-1][7:8], cosines[-1][7:8]
        pairs = list(zip(sines, cosines))
        sines += [s * by_cos + c * by_sin for s, c in pairs]
        cosines += [c * by_cos - s * by_sin for s, c in pairs]
    return jnp.concatenate(sines, axis=0), jnp.concatenate(cosines, axis=0)


def coords():
    b = lax.axis_index("batch")
    g = lax.axis_index("grid")
    return b // 2, g // 4, ((g // 2) % 2) * 2 + b % 2, g % 2


def device(x, y, z, core):
    return {"batch": x * 2 + z % 2, "grid": y * 4 + (z // 2) * 2 + core}


def remote(src, dst, sems, k, target):
    return pltpu.make_async_remote_copy(
        src_ref=src,
        dst_ref=dst,
        send_sem=sems.at[0, k],
        recv_sem=sems.at[1, k],
        device_id=target,
        device_id_type=MESH,
    )


def wait_bytes(ref, sem):
    pltpu.make_async_copy(ref, ref, sem).wait()


OFFSETS = sorted(
    itertools.product(range(4), repeat=3), key=lambda o: -sum(min(d, 4 - d) for d in o)
)


class Chips:
    def __init__(self):
        self.x, self.y, self.z, self.core = coords()
        self.rank = (self.x * 4 + self.y) * 4 + self.z
        self.odd = (self.x + self.y + self.z) % 2
        self.sibling = device(self.x, self.y, self.z, 1 - self.core)
        xs = [(self.x + d) % 4 for d in range(4)]
        ys = [(self.y + d) % 4 for d in range(4)]
        zs = [(self.z + d) % 4 for d in range(4)]
        ranks = [x * 16 for x in xs], [y * 4 for y in ys], zs
        batches = [x * 2 for x in xs], [z % 2 for z in zs]
        grids = [y * 4 + self.core for y in ys], [(z // 2) * 2 for z in zs]
        self.all = [
            (
                sum(o),
                (xs[o[0]], ys[o[1]], zs[o[2]]),
                ranks[0][o[0]] + ranks[1][o[1]] + ranks[2][o[2]],
                {"batch": batches[0][o[0]] + batches[1][o[2]], "grid": grids[0][o[1]] + grids[1][o[2]]},
            )
            for o in OFFSETS
        ]
        self.others = self.all[:-1]
        self.place = (self.x, self.y, self.z)


class Reducer:
    def __init__(self, chips, own, pair_send, pair_recv, send, recv, half, out, sems, counts):
        self.chips = chips
        self.own, self.pair_send, self.pair_recv = own, pair_send, pair_recv
        self.send, self.recv, self.half, self.out = send, recv, half, out
        self.sems, self.counts = sems, counts
        self.tiles = own.shape[1]
        self.readers = chips.others

    def by_parity(self, action):
        for odd in range(2):
            pl.when(self.chips.odd == odd)(functools.partial(action, odd))

    def place(self, rank, odd):
        return rank // 2

    def start_pair(self):
        self.pair_send[...] = self.own[1 - self.chips.core].astype(BF)
        remote(self.pair_send, self.pair_recv, self.sems, 0, self.chips.sibling).start()

    def start_scatter(self):
        chips = self.chips
        wait_bytes(self.pair_recv, self.sems.at[1, 0])
        self.send[...] = (self.own[chips.core] + self.pair_recv[...].astype(F32)).astype(BF)

        def go(odd):
            for k in range(self.counts[odd]):
                self.recv[k, chips.rank] = self.send[self.place(chips.rank, odd) + k]
            for turn, _, rank, target in chips.others:
                theirs = (odd + turn) % 2
                count = self.counts[theirs]
                if count:
                    src = self.send.at[pl.ds(self.place(rank, theirs), count)]
                    dst = self.recv.at[pl.ds(0, count), chips.rank]
                    remote(src, dst, self.sems, 1, target).start()

        self.by_parity(go)

    def start_gather(self):
        chips = self.chips

        def go(odd):
            count = self.counts[odd]
            if not count:
                return
            wait_bytes(self.recv.at[pl.ds(0, count), pl.ds(0, CHIPS - 1)], self.sems.at[1, 1])
            spot = self.place(chips.rank, odd)
            for k in range(count):
                self.half[spot + k] = jnp.sum(self.recv[k].astype(F32), axis=0).astype(BF)
            part = self.half.at[pl.ds(spot, count)]
            for *_, target in self.readers:
                remote(part, part, self.sems, 3, target).start()

        self.by_parity(go)

    def start_return(self):
        def go(odd):
            wait_bytes(self.pair_send.at[pl.ds(0, self.tiles - self.counts[odd])], self.sems.at[1, 3])

        self.by_parity(go)
        out = self.out.at[self.chips.core]
        remote(self.half, out, self.sems, 4, self.chips.sibling).start()
        pltpu.make_async_copy(self.half, out, self.sems.at[0, 5]).start()

    def sent(self, odd):
        count = self.counts[odd]
        wait_bytes(self.pair_send.at[pl.ds(0, self.tiles - count)], self.sems.at[0, 1])
        if count:
            wait_bytes(self.recv.at[pl.ds(0, count), pl.ds(0, CHIPS - 1)], self.sems.at[0, 3])

    def finish(self):
        wait_bytes(self.pair_send, self.sems.at[0, 0])
        self.by_parity(self.sent)
        wait_bytes(self.pair_send, self.sems.at[0, 4])
        wait_bytes(self.pair_send, self.sems.at[0, 5])
        wait_bytes(self.pair_recv, self.sems.at[1, 4])


CLASSES = ((0, 2), (1,))


def class_spot(place, axis):
    u, v = (c for k, c in enumerate(place) if k != axis)
    return 32 * axis + 8 * place[axis] + (u * 4 + v) // 2


class BranchReducer(Reducer):
    def start_scatter(self):
        chips = self.chips
        wait_bytes(self.pair_recv, self.sems.at[1, 0])
        self.send[...] = (self.own[chips.core] + self.pair_recv[...].astype(F32)).astype(BF)

        def go(odd):
            for k, axis in enumerate(CLASSES[odd]):
                self.recv[k, chips.rank] = self.send[class_spot(chips.place, axis)]
            for turn, place, _, target in chips.others:
                for k, axis in enumerate(CLASSES[(odd + turn) % 2]):
                    src, dst = self.send.at[class_spot(place, axis)], self.recv.at[k, chips.rank]
                    remote(src, dst, self.sems, 1, target).start()

        self.by_parity(go)

    def start_gather(self):
        chips = self.chips

        def go(odd):
            count = self.counts[odd]
            wait_bytes(self.recv.at[pl.ds(0, count), pl.ds(0, CHIPS - 1)], self.sems.at[1, 1])
            for k, axis in enumerate(CLASSES[odd]):
                spot = class_spot(chips.place, axis)
                self.half[spot] = jnp.sum(self.recv[k].astype(F32), axis=0).astype(BF)
                part = self.half.at[spot]
                for o, (*_, target) in zip(OFFSETS, chips.others):
                    if o[axis] == 0:
                        remote(part, part, self.sems, 3, target).start()

        self.by_parity(go)

    def start_line(self):
        def go(odd):
            wait_bytes(self.pair_send.at[pl.ds(0, 24 - self.counts[odd])], self.sems.at[1, 3])

        self.by_parity(go)
        for o, (*_, target) in zip(OFFSETS, self.chips.others):
            if o.count(0) == 2:
                axis = next(k for k in range(3) if o[k])
                part = self.half.at[pl.ds(32 * axis + 8 * self.chips.place[axis], 8)]
                remote(part, part, self.sems, 6, target).start()

    def start_return(self):
        wait_bytes(self.pair_send.at[pl.ds(0, 72)], self.sems.at[1, 6])
        out = self.out.at[self.chips.core]
        remote(self.half, out, self.sems, 4, self.chips.sibling).start()
        pltpu.make_async_copy(self.half, out, self.sems.at[0, 5]).start()

    def sent(self, odd):
        count = self.counts[odd]
        wait_bytes(self.pair_send.at[pl.ds(0, self.tiles - count)], self.sems.at[0, 1])
        wait_bytes(self.recv.at[pl.ds(0, count), pl.ds(0, 15)], self.sems.at[0, 3])
        wait_bytes(self.pair_send.at[pl.ds(0, 72)], self.sems.at[0, 6])


class PlaneReducer(Reducer):
    def __init__(self, chips, *refs):
        super().__init__(chips, *refs, (1, 1))
        self.readers = [other for o, other in zip(OFFSETS, chips.others) if o[0] == 0]

    def by_parity(self, action):
        action(0)

    def place(self, rank, odd):
        return rank % 16

    def sent(self, odd):
        wait_bytes(self.recv.at[0, pl.ds(0, CHIPS - 1)], self.sems.at[0, 1])
        wait_bytes(self.recv.at[0, pl.ds(0, len(self.readers))], self.sems.at[0, 3])


class SquareReducer:
    def __init__(self, chips, own, pair, recv, line, total, out, sems):
        self.chips, self.own, self.pair, self.recv, self.line = chips, own, pair, recv, line
        self.total, self.out, self.sems = total, out, sems

    def start_pair(self):
        remote(self.own, self.pair, self.sems, 0, self.chips.sibling).start()

    def start_scatter(self):
        wait_bytes(self.pair, self.sems.at[1, 0])
        slot = self.recv.at[self.chips.rank % 16]
        slot[...] = self.own[...] + self.pair[...]
        for o, (*_, target) in zip(OFFSETS, self.chips.others):
            if o[0] == 0:
                remote(slot, slot, self.sems, 1, target).start()

    def start_line(self):
        wait_bytes(self.recv.at[pl.ds(0, 15)], self.sems.at[1, 1])
        slot = self.line.at[self.chips.x]
        slot[...] = jnp.sum(self.recv[...], axis=0)
        for o, (*_, target) in zip(OFFSETS, self.chips.others):
            if o[1:] == (0, 0):
                remote(slot, slot, self.sems, 2, target).start()

    def start_return(self):
        wait_bytes(self.line.at[pl.ds(0, 3)], self.sems.at[1, 2])
        self.total[...] = (self.line[0] + self.line[1]) + (self.line[2] + self.line[3])
        pltpu.make_async_copy(self.total, self.out, self.sems.at[0, 3]).start()

    def finish(self):
        wait_bytes(self.own, self.sems.at[0, 0])
        wait_bytes(self.recv.at[pl.ds(0, 15)], self.sems.at[0, 1])
        wait_bytes(self.line.at[pl.ds(0, 3)], self.sems.at[0, 2])
        wait_bytes(self.total, self.sems.at[0, 3])


def tile_spots():
    singles, doubles = [], []
    for place in itertools.product(range(4), repeat=3):
        axes = CLASSES[sum(place) % 2]
        singles.append(class_spot(place, axes[0]))
        doubles += [class_spot(place, axis) for axis in axes[1:]]
    return singles, doubles


def step_kernel(
    grad_factor,
    samples_in, index_in, targets_in, w_in_in, w_mid_in, w_out_in, v_in_in, v_mid_in, v_out_in,
    branch_out, trunk_out, first_out, square_out,
    samples, index, targets, w_in, w_mid, w_out, v_in, v_mid, v_out,
    feats, t_one, t_two, basis, basis_grad, b_one, b_two, coeff, coeff_t, coeff_grad,
    squares,
    branch_own, branch_pair_send, branch_pair_recv, branch_send, branch_recv, branch_half,
    trunk_own, trunk_pair_send, trunk_pair_recv, trunk_send, trunk_recv, trunk_half,
    first_own, first_pair_send, first_pair_recv, first_send, first_recv, first_half,
    square_own, square_pair, square_recv, square_line, square_total,
    local_sems, target_sems, branch_sems, trunk_sems, first_sems, square_sems,
):
    samp, pts = targets.shape
    chunks = target_sems.shape[0]
    chunk = samp // chunks
    chips = Chips()
    branch = BranchReducer(
        chips, branch_own, branch_pair_send, branch_pair_recv, branch_send, branch_recv,
        branch_half, branch_out, branch_sems, (2, 1),
    )
    trunk = Reducer(
        chips, trunk_own, trunk_pair_send, trunk_pair_recv, trunk_send, trunk_recv,
        trunk_half, trunk_out, trunk_sems, (0, 1),
    )
    first = PlaneReducer(
        chips, first_own, first_pair_send, first_pair_recv, first_send, first_recv,
        first_half, first_out, first_sems,
    )
    square = SquareReducer(
        chips, square_own, square_pair, square_recv, square_line, square_total, square_out,
        square_sems,
    )

    loads = []
    for k, (src, dst) in enumerate(
        (
            (index_in, index), (v_in_in, v_in), (v_mid_in, v_mid), (v_out_in, v_out),
            (w_in_in, w_in), (w_mid_in, w_mid), (w_out_in, w_out), (samples_in, samples),
        )
    ):
        copy = pltpu.make_async_copy(src, dst, local_sems.at[k])
        copy.start()
        loads.append(copy)
    target_loads = []
    for k in range(chunks):
        rows = pl.ds(k * chunk, chunk)
        copy = pltpu.make_async_copy(targets_in.at[rows], targets.at[rows], target_sems.at[k])
        copy.start()
        target_loads.append(copy)

    barrier = pltpu.get_barrier_semaphore()

    def greet(target):
        pl.semaphore_signal(barrier, inc=1, device_id=target, device_id_type=MESH)

    greet(chips.sibling)
    for *_, target in chips.others:
        greet(target)

    for k in range(4):
        loads[k].wait()
    quarter = feats.shape[0] // 4
    v_in_t, v_mid_t, v_out_t = v_in[...].T, v_mid[...].T, v_out[...].T
    wide = 1024
    block = 512
    blocks = pts // block

    def trunk_feats(p):
        cols = pl.ds(p * block, block)
        for axis in range(2):
            turns = (2.0 * index[axis : axis + 1, cols].astype(F32) + 1.0) * (0.25 / GRID_SIDE)
            sines, cosines = waves(turns, quarter)
            base = 2 * axis * quarter
            feats[base : base + quarter, cols] = sines.astype(BF)
            feats[base + quarter : base + 2 * quarter, cols] = cosines.astype(BF)

    def trunk_one(p):
        cols = pl.ds(p * block, block)
        t_one[:, cols] = jnp.tanh(dot(v_in_t, feats[:, cols], 1, 0)).astype(BF)

    def trunk_two(p):
        cols = pl.ds(p * block, block)
        t_two[:, cols] = jnp.tanh(dot(v_mid_t, t_one[:, cols], 1, 0)).astype(BF)

    def trunk_basis(p):
        cols = pl.ds(p * block, block)
        basis[:, cols] = dot(v_out_t, t_two[:, cols], 1, 0).astype(BF)

    quarter_rows = samp // 4

    def branch_one(k):
        rows = pl.ds(k * quarter_rows, quarter_rows)
        b_one[rows, :] = jnp.tanh(dot(samples[rows, :], w_in[...], 1, 0)).astype(BF)

    def branch_two(k):
        rows = pl.ds(k * quarter_rows, quarter_rows)
        b_two[rows, :] = jnp.tanh(dot(b_one[rows, :], w_mid[...], 1, 0)).astype(BF)

    def branch_coeff(k):
        rows = pl.ds(k * quarter_rows, quarter_rows)
        coeff[rows, :] = dot(b_two[rows, :], w_out[...], 1, 0).astype(BF)

    stages = (trunk_feats, trunk_one, trunk_two, trunk_basis)
    branch_stages = (branch_one, branch_two, branch_coeff)
    branch_from = 5
    for step in range(blocks + len(stages) - 1):
        if step == branch_from:
            for k in range(4, 8):
                loads[k].wait()
        for lag, stage in enumerate(stages):
            if 0 <= step - lag < blocks:
                stage(step - lag)
        for lag, stage in enumerate(branch_stages):
            if 0 <= step - branch_from - lag < 4:
                stage(step - branch_from - lag)
    coeff_t[...] = coeff[...].T

    squares[...] = jnp.zeros_like(squares)
    for k in range(chunks):
        rows = pl.ds(k * chunk, chunk)
        target_loads[k].wait()
        scaled = coeff[rows, :] * jnp.asarray(1.0 / 16.0, BF)
        for p in range(0, pts, wide):
            cols = pl.ds(p, wide)
            residual = dot(scaled, basis[:, cols], 1, 0) - targets[rows, cols].astype(F32)
            targets[rows, cols] = (residual * grad_factor).astype(BF)
            squared = residual * residual
            squares[...] += jnp.sum(squared.reshape(chunk // 8, 8, wide), axis=0)
        coeff_grad[rows, :] = dot(targets[rows, :], basis[...], 1, 1).astype(BF)

    grad = coeff_grad[...]
    part_out = dot(b_two[...], grad, 0, 0)
    slope = 1.0 - jnp.square(b_two[...].astype(F32))
    back_two = (dot(grad, w_out[...], 1, 1) * slope).astype(BF)
    part_mid = dot(b_one[...], back_two, 0, 0)
    slope = 1.0 - jnp.square(b_one[...].astype(F32))
    back_one = (dot(back_two, w_mid[...], 1, 1) * slope).astype(BF)
    part_in = dot(samples[...], back_one, 0, 0)
    square_own[...] = jnp.sum(jnp.sum(squares[...].reshape(8, wide // 128, 128), axis=1), axis=0, keepdims=True)

    def pack(own, part, core, spots, row):
        for k, spot in enumerate(spots):
            strip = part[row + 8 * k : row + 8 * k + 8]
            own[core, spot, 0:8] = strip[:, :128]
            own[core, spot, 8:16] = strip[:, 128:]

    singles, doubles = tile_spots()
    for c in range(2):
        pack(branch_own, part_in, c, singles, c * 512)
        pack(branch_own, part_mid, c, doubles[:16], c * 128)
        pack(branch_own, part_out, c, doubles[16:], c * 128)

    pl.semaphore_wait(barrier, CHIPS)
    branch.start_pair()
    square.start_pair()

    for p in range(0, pts, wide):
        cols = pl.ds(p, wide)
        basis_grad[:, cols] = dot(coeff_t[...], targets[:, cols], 1, 0).astype(BF)
        if p == wide:
            branch.start_scatter()
            square.start_scatter()

    def pack_trunk(own, part, spot):
        for c in range(2):
            pack(own, part, c, range(spot, spot + 16), c * 128)

    def back(weight, grad, hidden, result):
        for p in range(0, pts, wide):
            cols = pl.ds(p, wide)
            slope = 1.0 - jnp.square(hidden[:, cols].astype(F32))
            result[:, cols] = (dot(weight[...], grad[:, cols], 1, 0) * slope).astype(BF)

    back_two_t, back_one_t = basis, basis_grad
    pack_trunk(trunk_own, dot(t_two[...], basis_grad[...], 1, 1), 0)
    back(v_out, basis_grad, t_two, back_two_t)
    pack_trunk(trunk_own, dot(t_one[...], back_two_t[...], 1, 1), 16)
    trunk.start_pair()
    back(v_mid, back_two_t, t_one, back_one_t)
    trunk.start_scatter()
    pack_trunk(first_own, dot(feats[...], back_one_t[...], 1, 1), 0)
    first.start_pair()
    first.start_scatter()

    square.start_line()
    branch.start_gather()
    trunk.start_gather()
    square.start_return()
    first.start_gather()
    branch.start_line()
    trunk.start_return()
    first.start_return()
    branch.start_return()
    trunk.finish()
    branch.finish()
    first.finish()
    square.finish()


def spread_kernel(
    loss_scale, branch_in, trunk_in, first_in, square_in, g_w_in, g_w_mid, g_w_out, g_v_in, g_v_mid, g_v_out, loss_out,
    branch, trunk, first, square, loss, w_in, w_mid, w_out, v_in, v_mid, v_out, in_sems, out_sems,
):
    loads = [
        pltpu.make_async_copy(src, dst, in_sems.at[k])
        for k, (src, dst) in enumerate(
            (
                (branch_in.at[0], branch.at[0]), (branch_in.at[1], branch.at[1]),
                (trunk_in, trunk), (first_in, first), (square_in, square),
            )
        )
    ]
    for load in loads:
        load.start()
    stores = []

    def put(src, c, spots, held, out):
        rows = 8 * len(spots)
        for k, spot in enumerate(spots):
            tile = src[c, spot].astype(F32)
            row = c * rows + 8 * k
            held[row : row + 8, 0:128] = tile[:8]
            held[row : row + 8, 128:256] = tile[8:]
        span = pl.ds(c * rows, rows)
        store = pltpu.make_async_copy(held.at[span], out.at[span], out_sems.at[len(stores)])
        store.start()
        stores.append(store)

    singles, doubles = tile_spots()
    for c in range(2):
        loads[c].wait()
        put(branch, c, singles, w_in, g_w_in)
        put(branch, c, doubles[:16], w_mid, g_w_mid)
        put(branch, c, doubles[16:], w_out, g_w_out)
    loads[2].wait()
    loads[3].wait()
    for c in range(2):
        put(trunk, c, range(16), v_out, g_v_out)
        put(trunk, c, range(16, 32), v_mid, g_v_mid)
        put(first, c, range(16), v_in, g_v_in)
    loads[4].wait()
    loss[...] = jnp.sum(square[...], keepdims=True) * loss_scale
    stores.append(pltpu.make_async_copy(loss, loss_out, out_sems.at[len(stores)]))
    stores[-1].start()
    for store in stores:
        store.wait()


def on_device(samples, point_index, targets, w_in, w_mid, w_out, v_in, v_mid, v_out):
    samp, pts = targets.shape
    total_cells = samp * lax.axis_size("batch") * pts * lax.axis_size("grid")
    sensors, hidden = w_in.shape
    grad_factor = 64.0 / math.sqrt(total_cells) * w_out.shape[1] ** (-0.5)
    chunks = 2
    any_spec = pl.BlockSpec(memory_space=pl.ANY)
    inputs = (samples, point_index, targets, w_in, w_mid, w_out, v_in, v_mid, v_out)
    v = pltpu.VMEM
    scratch = [v(a.shape, a.dtype) for a in inputs]
    scratch += [v((hidden, pts), BF)] * 5
    scratch += [v((samp, hidden), BF)] * 3 + [v((hidden, samp), BF), v((samp, hidden), BF)]
    scratch += [v((8, 1024), F32)]
    for tiles, most in ((BRANCH_TILES, 2), (TRUNK_TILES, 1), (FIRST_TILES, 1)):
        scratch += [
            v((2, tiles, *TILE), F32),
            v((tiles, *TILE), BF),
            v((tiles, *TILE), BF),
            v((tiles, *TILE), BF),
            v((most, CHIPS, *TILE), BF),
            v((tiles, *TILE), BF),
        ]
    scratch += [v((1, 128), F32), v((1, 128), F32), v((16, 1, 128), F32), v((4, 1, 128), F32)]
    scratch += [v((1, 128), F32)]
    scratch += [
        pltpu.SemaphoreType.DMA((8,)),
        pltpu.SemaphoreType.DMA((chunks,)),
        pltpu.SemaphoreType.DMA((2, 7)),
        pltpu.SemaphoreType.DMA((2, 6)),
        pltpu.SemaphoreType.DMA((2, 6)),
        pltpu.SemaphoreType.DMA((2, 4)),
    ]
    branch, trunk, first, square = pl.pallas_call(
        functools.partial(step_kernel, grad_factor),
        out_shape=(
            jax.ShapeDtypeStruct((2, BRANCH_TILES, *TILE), BF),
            jax.ShapeDtypeStruct((2, TRUNK_TILES, *TILE), BF),
            jax.ShapeDtypeStruct((2, FIRST_TILES, *TILE), BF),
            jax.ShapeDtypeStruct((1, 128), F32),
        ),
        in_specs=[any_spec] * 9,
        out_specs=[any_spec] * 4,
        scratch_shapes=scratch,
        compiler_params=pltpu.CompilerParams(
            collective_id=0, has_side_effects=True, vmem_limit_bytes=58 << 20
        ),
        name="deeponet_step",
    )(*inputs)
    shapes = [(sensors, hidden)] + [(hidden, hidden)] * 5 + [(1, 1)]
    outs = pl.pallas_call(
        functools.partial(spread_kernel, 1.0 / (2.0 * total_cells)),
        out_shape=[jax.ShapeDtypeStruct(s, F32) for s in shapes],
        in_specs=[any_spec] * 4,
        out_specs=[any_spec] * 7,
        scratch_shapes=[v((2, n, *TILE), BF) for n in (BRANCH_TILES, TRUNK_TILES, FIRST_TILES)]
        + [v((1, 128), F32), v((1, 1), F32)]
        + [v(s, F32) for s in shapes[:6]]
        + [pltpu.SemaphoreType.DMA((5,)), pltpu.SemaphoreType.DMA((13,))],
        compiler_params=pltpu.CompilerParams(vmem_limit_bytes=60 << 20),
        name="spread_gradients",
    )(branch, trunk, first, square)
    return (*outs[:6], outs[6].reshape(()))


def solution(mesh):
    placed = (P("batch", None), P(None, "grid"), P("batch", "grid"), P(), P(), P(), P(), P(), P())
    return jax.shard_map(
        on_device,
        mesh=mesh,
        in_specs=placed,
        out_specs=(P(), P(), P(), P(), P(), P(), P()),
        check_vma=False,
    )
```
